512 devices in a mesh: row: 16 (over x, y), col: 16 (over z_lo, core), cfg: 2 (over z_hi).
Axes of the slice: x: 4, y: 4, z: 16 (z_hi: 2, z_lo: 8; z = z_hi * 8 + z_lo), core: 2. Of those that a mesh axis runs over, the one named last changes fastest.
Arguments:
- features: bfloat16 [2, 192, 1024, 320], P('cfg', 'row', 'col'), may hold values from -6 to 6
- latent: float32 [4, 192, 1024], P('cfg', 'row', 'col'), may hold values from -6 to 6
- conv_weight: bfloat16 [2, 2, 9, 320, 320], replicated, may hold values from -0.109375 to 0.109375
- conv_bias: float32 [2, 2, 320], replicated, may hold values from -2 to 2
- norm_gain: float32 [5, 320], replicated, may hold values from 0.5 to 1.5
- norm_shift: float32 [5, 320], replicated, may hold values from -2 to 2
- emb_shift: float32 [2, 2, 320], P('cfg'), may hold values from -5 to 5
- stale_mean: float32 [2, 5, 32], P('cfg'), may hold values from -2 to 2
- stale_var: float32 [2, 5, 32], P('cfg'), may hold values from 0.3 to 3
- out_weight: bfloat16 [9, 320, 4], replicated, may hold values from -0.109375 to 0.109375
- out_bias: float32 [4], replicated, may hold values from -2 to 2
- guidance: float32 [1], replicated, may hold values from 2 to 6
- timestep: int32 [1], replicated, may hold values from 0 to 49
- coeffs: float32 [50, 2], replicated, may hold values from 0.5 to 1.5
Outputs:
- latent_next: float32 [4, 192, 1024], P('cfg', 'row', 'col')
The draws below stay inside these ranges and needn't reach their ends.
Inputs may be any that keep to these rules, and one draw needn't show every extreme that they name: `timestep`: the row of coeffs used in this step.
All inputs are finite; a program needn't handle non-finite values.
Results may differ from the reference program's by a relative error of at most 0.02.
Values may be sent and summed in bfloat16 or wider, within the bound.
A program may use at most 64 MiB of HBM per device.

```python
import math
import jax
import jax.numpy as jnp
from jax import lax

C = 320
GROUPS = 32
LAT = 4
BLOCKS = 2
STEPS = 50
NORMS = 5
NX = 192
NY = 1024


def shard_levels(key, extent, split, smallest, high):
    def one(position, blocks):
        heights = jax.random.uniform(jax.random.fold_in(jax.random.fold_in(key, 6), position), (blocks,), jnp.float32, smallest / len(split), high / len(split))
        return jnp.repeat(jnp.exp(heights), extent[position] // blocks).reshape((-1,) + (1,) * (len(extent) - position - 1))

    loudness = one(*split[0])
    for cut in split[1:]:
        loudness = loudness * one(*cut)
    return loudness


def bell_draw(key, shape, spread, bound, split=(), held_as=jnp.bfloat16):
    values = jax.random.normal(key, shape, jnp.float32) * spread
    if len(split) > 0:
        values = shard_levels(key, shape, split, -0.22, 0.18) * values
    return jnp.clip(values, min=-bound, max=bound).astype(held_as)


def setup_inputs(seed: int = 0) -> dict:
    key_of = jax.random.split(jax.random.key(seed), 15)
    features = bell_draw(key_of[0], (2, NX, NY, C), 1.0, 6.0, ((0, 2), (1, 16), (2, 16)))
    latent = bell_draw(key_of[1], (LAT, NX, NY), 1.0, 6.0, ((0, 2), (1, 16), (2, 16)), jnp.float32)
    conv_weight = bell_draw(key_of[2], (BLOCKS, 2, 9, C, C), (9 * C) ** -0.5, 0.109375)
    conv_bias = bell_draw(key_of[3], (BLOCKS, 2, C), 0.3, 2.0, (), jnp.float32)
    norm_gain = jnp.clip(1.0 + 0.1 * jax.random.normal(key_of[4], (NORMS, C), jnp.float32), 0.5, 1.5)
    norm_shift = bell_draw(key_of[5], (NORMS, C), 0.3, 2.0, (), jnp.float32)
    emb_shift = bell_draw(key_of[6], (2, BLOCKS, C), 1.0, 5.0, ((0, 2),), jnp.float32)
    stale_mean = bell_draw(key_of[7], (2, NORMS, GROUPS), 0.3, 2.0, ((0, 2),), jnp.float32)
    stale_var = jnp.clip(jnp.exp(math.log(3.0) - 2.3025851 * jax.random.uniform(key_of[8], (2, NORMS, GROUPS), jnp.float32) ** shard_levels(key_of[8], (2, NORMS, GROUPS), ((0, 2),), -0.2, 0.2)), 0.3, 3.0)
    out_weight = bell_draw(key_of[9], (9, C, LAT), (9 * C) ** -0.5, 0.109375)
    out_bias = bell_draw(key_of[10], (LAT,), 0.3, 2.0, (), jnp.float32)
    guidance = jnp.clip(jax.random.uniform(key_of[11], (1,), jnp.float32, 2.0, 6.0), 2.0, 6.0)
    timestep = jax.random.randint(key_of[12], (1,), 0, STEPS).astype(jnp.int32)
    coeffs = jnp.clip(jax.random.uniform(key_of[13], (STEPS, 2), jnp.float32, 0.5, 1.5), 0.5, 1.5)
    return {"features": features, "latent": latent, "conv_weight": conv_weight, "conv_bias": conv_bias, "norm_gain": norm_gain, "norm_shift": norm_shift, "emb_shift": emb_shift, "stale_mean": stale_mean, "stale_var": stale_var, "out_weight": out_weight, "out_bias": out_bias, "guidance": guidance, "timestep": timestep, "coeffs": coeffs}


norm_eps = 1e-05

def activate(values, index, group_mean, group_var, norm_gain, norm_shift):
    channels = values.shape[-1]
    repeat_by = channels // group_mean.shape[-1]
    centre = jnp.repeat(group_mean[index], repeat_by)
    scaling = jnp.repeat(lax.rsqrt(group_var[index] + norm_eps), repeat_by)
    normed = (values.astype(jnp.float32) - centre) * scaling * norm_gain[index] + norm_shift[index]
    return jax.nn.silu(normed)

def conv_valid(padded, kernel):
    row_count = padded.shape[0] - 2
    col_count = padded.shape[1] - 2
    channels = padded.shape[2]
    summed = None
    for tap_index in range(9):
        tap_row, tap_col = divmod(tap_index, 3)
        window = padded[tap_row:tap_row + row_count, tap_col:tap_col + col_count].reshape(row_count * col_count, channels)
        product = jnp.dot(window, kernel[tap_index], preferred_element_type=jnp.float32)
        summed = product if summed is None else summed + product
    return summed.reshape(row_count, col_count, kernel.shape[2])

def pad_zero(field):
    return jnp.pad(field, ((1, 1), (1, 1), (0, 0)))

def reference(features, latent, conv_weight, conv_bias, norm_gain, norm_shift, emb_shift, stale_mean, stale_var, out_weight, out_bias, guidance, timestep, coeffs):
    predictions = []
    for branch in range(2):
        hidden = features[branch]
        group_mean = stale_mean[branch]
        group_var = stale_var[branch]
        for block_index in range(BLOCKS):
            first_act = activate(hidden, 2 * block_index, group_mean, group_var, norm_gain, norm_shift).astype(jnp.bfloat16)
            inner_sum = conv_valid(pad_zero(first_act), conv_weight[block_index, 0]) + conv_bias[block_index, 0] + emb_shift[branch, block_index]
            second = activate(inner_sum, 2 * block_index + 1, group_mean, group_var, norm_gain, norm_shift).astype(jnp.bfloat16)
            conv_two = conv_valid(pad_zero(second), conv_weight[block_index, 1]) + conv_bias[block_index, 1]
            hidden = (hidden.astype(jnp.float32) + conv_two).astype(jnp.bfloat16)
        final_act = activate(hidden, 2 * BLOCKS, group_mean, group_var, norm_gain, norm_shift).astype(jnp.bfloat16)
        noise_pred = conv_valid(pad_zero(final_act), out_weight) + out_bias
        predictions.append(jnp.transpose(noise_pred, (2, 0, 1)))
    uncond = predictions[0]
    conditioned = predictions[1]
    guided = uncond + guidance[0] * (conditioned - uncond)
    step_coef = coeffs[timestep[0]]
    return step_coef[0] * latent + step_coef[1] * guided
```

```python
import jax
import jax.numpy as jnp
from jax import lax
from jax.experimental import pallas as pl
from jax.experimental.pallas import tpu as pltpu
from jax.sharding import PartitionSpec as P

MESH = pl.DeviceIdType.MESH
BF, F32 = jnp.bfloat16, jnp.float32

C = 320
GROUPS = 32
ROWS, COLS = 12, 64
HALO = 5
WIDE = COLS + 2 * HALO
TALL = ROWS + 2 * HALO
STRIP = 16
STAGE = COLS + 2 * STRIP
STEP = WIDE + 1
TILE = 256
TILES = (6, 6, 5, 5)
GRID_ROWS, GRID_COLS = 16, 16
NORM_EPS = 1e-05

A_COL, B_COL, BIAS_COL = 0, 5, 10


def exact_parts(value):
    high = value.astype(BF).astype(F32)
    mid = (value - high).astype(BF).astype(F32)
    return high, mid, value - high - mid


def kernel(
    features,
    weight,
    latent,
    bias,
    gain,
    shift,
    emb,
    mean,
    var,
    out_weight,
    out_bias,
    guidance,
    timestep,
    coeffs,
    out,
    stage,
    wraw,
    wflat,
    patches,
    act_a,
    act_b,
    hid_a,
    hid_b,
    params,
    pcols,
    masks,
    wout,
    taps,
    eps,
    partner,
    load_sem,
    wsem,
    send_sem,
    recv_sem,
    cfg_send,
    cfg_recv,
):
    row, col, cfg = lax.axis_index("row"), lax.axis_index("col"), lax.axis_index("cfg")
    has = {
        (-1, 0): row > 0,
        (1, 0): row < GRID_ROWS - 1,
        (0, -1): col > 0,
        (0, 1): col < GRID_COLS - 1,
    }
    for dr in (-1, 1):
        for dc in (-1, 1):
            has[dr, dc] = has[dr, 0] & has[0, dc]
    sides = list(has)

    edge = (row == 0) | (row == GRID_ROWS - 1) | (col == 0) | (col == GRID_COLS - 1)

    @pl.when(edge)
    def _():
        stage[...] = jnp.zeros_like(stage)

    barrier = pltpu.get_barrier_semaphore()
    for dr, dc in sides:

        @pl.when(has[dr, dc])
        def _(dr=dr, dc=dc):
            pl.semaphore_signal(
                barrier, inc=1, device_id={"row": row + dr, "col": col + dc}, device_id_type=MESH
            )

    pl.semaphore_signal(barrier, inc=1, device_id={"cfg": 1 - cfg}, device_id_type=MESH)

    own = pltpu.make_async_copy(
        features.at[0], stage.at[pl.ds(HALO, ROWS), pl.ds(STRIP, COLS)], load_sem
    )
    own.start()
    loads = []
    for n in range(4):
        load = pltpu.make_async_copy(weight.at[n // 2, n % 2], wraw.at[n], wsem.at[n])
        load.start()
        loads.append(load)

    groups = lax.broadcasted_iota(jnp.int32, (GROUPS, C), 0)
    channels = lax.broadcasted_iota(jnp.int32, (GROUPS, C), 1)
    lowest = groups * (C // GROUPS)
    spread = jnp.where((channels >= lowest) & (channels < lowest + C // GROUPS), 1.0, 0.0).astype(F32)

    def to_channels(value):
        total = None
        for part in exact_parts(value):
            term = jnp.dot(part, spread, preferred_element_type=F32)
            total = term if total is None else total + term
        return total

    scale = to_channels(lax.rsqrt(var[0] + NORM_EPS)) * gain[...]
    offset = shift[...] - to_channels(mean[0]) * scale
    params[...] = jnp.zeros_like(params)
    for n in range(5):
        add = offset[n : n + 1]
        if n in (1, 3):
            k = n // 2
            add = add + scale[n : n + 1] * (bias[k, 0:1] + emb[0, k : k + 1])
        params[A_COL + n : A_COL + n + 1, 0:C] = 0.5 * scale[n : n + 1]
        params[B_COL + n : B_COL + n + 1, 0:C] = 0.5 * add
    for k in range(2):
        params[BIAS_COL + k : BIAS_COL + k + 1, 0:C] = bias[k, 1:2]
    pcols[...] = jnp.transpose(params[...])

    for t in range(9):
        padded = jnp.concatenate([out_weight[t].astype(F32), jnp.zeros((C, 4), F32)], axis=1)
        wout[8 * t : 8 * t + 8, :] = jnp.transpose(padded)

    for n in range(5):
        cell = lax.broadcasted_iota(jnp.int32, (8, masks.shape[2]), 1) + n * STEP
        cell_row = lax.shift_right_logical(cell * 28340, 21)
        cell_col = cell - cell_row * WIDE
        grid_row = cell_row + (row * ROWS - HALO)
        grid_col = cell_col + (col * COLS - HALO)
        inside = (
            (grid_row >= 0)
            & (grid_row < GRID_ROWS * ROWS)
            & (grid_col >= 0)
            & (grid_col < GRID_COLS * COLS)
        )
        masks[n] = jnp.where(inside, 1.0, 0.0).astype(F32)

    eye_row = lax.broadcasted_iota(jnp.int32, (C, C), 0)
    eye_col = lax.broadcasted_iota(jnp.int32, (C, C), 1)
    eye = jnp.where(eye_row == eye_col, 1.0, 0.0).astype(BF)

    def flipped(value):
        return lax.dot_general(
            eye, value, (((1,), (1,)), ((), ())), preferred_element_type=F32
        ).astype(BF)

    arrivals = sum(jnp.where(has[s], 1, 0) for s in sides) + 1
    pl.semaphore_wait(barrier, arrivals)

    row_src = {-1: pl.ds(0, HALO), 0: pl.ds(0, ROWS), 1: pl.ds(ROWS - HALO, HALO)}
    row_dst = {-1: pl.ds(HALO + ROWS, HALO), 0: pl.ds(HALO, ROWS), 1: pl.ds(0, HALO)}
    col_src = {-1: pl.ds(0, STRIP), 0: pl.ds(0, COLS), 1: pl.ds(COLS - STRIP, STRIP)}
    col_dst = {-1: pl.ds(STRIP + COLS, STRIP), 0: pl.ds(STRIP, COLS), 1: pl.ds(0, STRIP)}
    copies = {}
    for n, (dr, dc) in enumerate(sides):
        copy = pltpu.make_async_remote_copy(
            src_ref=features.at[0, row_src[dr], col_src[dc]],
            dst_ref=stage.at[row_dst[dr], col_dst[dc]],
            send_sem=send_sem.at[n],
            recv_sem=recv_sem.at[n],
            device_id={"row": row + dr, "col": col + dc},
            device_id_type=MESH,
        )
        copies[dr, dc] = copy

        @pl.when(has[dr, dc])
        def _(copy=copy):
            copy.start()

    for n in range(4):
        loads[n].wait()

        @pl.loop(0, 1)
        def _(_, n=n):
            wflat[n] = flipped(wraw[n].reshape(9 * C, C))

    own.wait()
    for dr, dc in sides:
        copy = copies[dr, dc]

        @pl.when(has[-dr, -dc])
        def _(copy=copy):
            copy.wait_recv()

    def silu(values, norm, frame, first):
        size = values.shape[1]
        half = values * pcols[0:C, A_COL + norm : A_COL + norm + 1] + pcols[
            0:C, B_COL + norm : B_COL + norm + 1
        ]
        masked = half * masks[frame, 0:1, first : first + size]
        return (masked * (1.0 + jnp.tanh(half))).astype(BF)

    for first, count in ((HALO, ROWS), (0, HALO), (HALO + ROWS, HALO)):
        turned = flipped(stage[first : first + count].reshape(count * STAGE, C))
        for n in range(count):
            begin = n * STAGE + STRIP - HALO
            hid_a[:, (first + n) * WIDE : (first + n + 1) * WIDE] = turned[:, begin : begin + WIDE]
    hid_a[:, TALL * WIDE :] = jnp.zeros((C, hid_a.shape[1] - TALL * WIDE), BF)
    for n in range(hid_a.shape[1] // TILE):
        part = slice(n * TILE, (n + 1) * TILE)
        act_a[:, part] = silu(hid_a[:, part].astype(F32), 0, 0, n * TILE)

    def conv(layer, source, finish):
        size = TILES[layer] * TILE
        for p in range(3):
            for q in range(3):
                tap = 3 * p + q
                patches[tap * C : (tap + 1) * C, 0:size] = source[:, p * WIDE + q : p * WIDE + q + size]
        for n in range(TILES[layer]):
            part = slice(n * TILE, (n + 1) * TILE)
            finish(part, jnp.dot(wflat[layer], patches[:, part], preferred_element_type=F32))

    def inner(layer, dest):
        def finish(part, total):
            dest[:, part] = silu(total, layer + 1, layer + 1, part.start)

        return finish

    def outer(layer, before, after, dest):
        k = layer // 2

        def finish(part, total):
            skip = before[:, part.start + 2 * STEP : part.stop + 2 * STEP].astype(F32)
            hidden = (skip + (total + pcols[0:C, BIAS_COL + k : BIAS_COL + k + 1])).astype(BF)
            if after is not None:
                after[:, part] = hidden
            dest[:, part] = silu(hidden.astype(F32), layer + 1, layer + 1, part.start)

        return finish

    conv(0, act_a, inner(0, act_b))
    conv(1, act_b, outer(1, hid_a, hid_b, act_a))
    conv(2, act_a, inner(2, act_b))
    conv(3, act_b, outer(3, hid_b, None, act_a))

    size = eps.shape[2]
    taps[...] = jnp.dot(wout[...].astype(BF), act_a[:, 0 : taps.shape[1]], preferred_element_type=F32)
    total = None
    for p in range(3):
        for q in range(3):
            t = 3 * p + q
            begin = p * WIDE + q
            term = taps[8 * t : 8 * t + 8, begin : begin + size]
            total = term if total is None else total + term
    for o in range(4):
        eps[o // 2, o % 2 : o % 2 + 1, :] = total[o : o + 1] + out_bias[o]

    swap = pltpu.make_async_remote_copy(
        src_ref=eps.at[1 - cfg],
        dst_ref=partner,
        send_sem=cfg_send,
        recv_sem=cfg_recv,
        device_id={"cfg": 1 - cfg},
        device_id_type=MESH,
    )
    swap.start()
    for dr, dc in sides:
        copy = copies[dr, dc]

        @pl.when(has[dr, dc])
        def _(copy=copy):
            copy.wait_send()

    swap.wait()
    mine, other = eps[cfg], partner[...]
    uncond = jnp.where(cfg == 1, other, mine)
    cond = jnp.where(cfg == 1, mine, other)
    guided = uncond + guidance[0] * (cond - uncond)
    step = timestep[0]
    c_latent, c_guided = coeffs[step, 0], coeffs[step, 1]
    for n in range(ROWS):
        out[:, n, :] = c_latent * latent[:, n, :] + c_guided * guided[:, n * WIDE : n * WIDE + COLS]


def per_device(
    features,
    latent,
    conv_weight,
    conv_bias,
    norm_gain,
    norm_shift,
    emb_shift,
    stale_mean,
    stale_var,
    out_weight,
    out_bias,
    guidance,
    timestep,
    coeffs,
):
    hbm = pl.BlockSpec(memory_space=pl.ANY)
    vmem = pl.BlockSpec(memory_space=pltpu.VMEM)
    smem = pl.BlockSpec(memory_space=pltpu.SMEM)
    dma = pltpu.SemaphoreType.DMA
    lanes = 1792
    return pl.pallas_call(
        kernel,
        out_shape=jax.ShapeDtypeStruct(latent.shape, F32),
        in_specs=[hbm, hbm] + [vmem] * 8 + [smem] * 4,
        out_specs=vmem,
        scratch_shapes=[
            pltpu.VMEM((TALL, STAGE, C), BF),
            pltpu.VMEM((4, 9, C, C), BF),
            pltpu.VMEM((4, C, 9 * C), BF),
            pltpu.VMEM((9 * C, TILES[0] * TILE), BF),
            pltpu.VMEM((C, lanes), BF),
            pltpu.VMEM((C, lanes), BF),
            pltpu.VMEM((C, lanes), BF),
            pltpu.VMEM((C, lanes), BF),
            pltpu.VMEM((128, 384), F32),
            pltpu.VMEM((384, 128), F32),
            pltpu.VMEM((5, 8, lanes), F32),
            pltpu.VMEM((72, C), F32),
            pltpu.VMEM((72, 1152), F32),
            pltpu.VMEM((2, 2, 896), F32),
            pltpu.VMEM((2, 896), F32),
            dma,
            dma((4,)),
            dma((8,)),
            dma((8,)),
            dma,
            dma,
        ],
        compiler_params=pltpu.CompilerParams(
            collective_id=0, has_side_effects=True, vmem_limit_bytes=58 * 2**20
        ),
        cost_estimate=pl.CostEstimate(
            flops=12 * 10**9, bytes_accessed=10 * 2**20, transcendentals=2 * 10**6
        ),
    )(
        features,
        conv_weight,
        latent,
        conv_bias,
        norm_gain,
        norm_shift,
        emb_shift,
        stale_mean,
        stale_var,
        out_weight,
        out_bias,
        guidance,
        timestep,
        coeffs,
    )


def solution(mesh):
    return jax.shard_map(
        per_device,
        mesh=mesh,
        in_specs=(
            P("cfg", "row", "col", None),
            P("cfg", "row", "col"),
            P(),
            P(),
            P(),
            P(),
            P("cfg", None, None),
            P("cfg", None, None),
            P("cfg", None, None),
            P(),
            P(),
            P(),
            P(),
            P(),
        ),
        out_specs=P("cfg", "row", "col"),
        check_vma=False,
    )
```

```python
import jax
import jax.numpy as jnp
from jax import lax
from jax.experimental import pallas as pl
from jax.experimental.pallas import tpu as pltpu
from jax.sharding import PartitionSpec as P

MESH = pl.DeviceIdType.MESH
BF, F32 = jnp.bfloat16, jnp.float32

C = 320
GROUPS = 32
ROWS, COLS = 12, 64
HALO = 5
WIDE = COLS + 2 * HALO
TALL = ROWS + 2 * HALO
STRIP = 16
STAGE = COLS + 2 * STRIP
STEP = WIDE + 1
TILE = 256
LANES = 128
TILES = (6, 6, 5, 5)
GRID_ROWS, GRID_COLS = 16, 16
NORM_EPS = 1e-05

A_COL, B_COL, BIAS_COL = 0, 5, 10


def exact_parts(value):
    high = value.astype(BF).astype(F32)
    mid = (value - high).astype(BF).astype(F32)
    return high, mid, value - high - mid


def kernel(
    features,
    weight,
    latent,
    bias,
    gain,
    shift,
    emb,
    mean,
    var,
    out_weight,
    out_bias,
    guidance,
    timestep,
    coeffs,
    out,
    stage,
    wraw,
    wflat,
    patches,
    act_a,
    act_b,
    hid_a,
    hid_b,
    hid_s,
    params,
    pcols,
    masks,
    wout,
    taps,
    eps,
    partner,
    load_sem,
    wsem,
    send_sem,
    recv_sem,
    cfg_send,
    cfg_recv,
):
    row, col, cfg = lax.axis_index("row"), lax.axis_index("col"), lax.axis_index("cfg")
    has = {
        (-1, 0): row > 0,
        (1, 0): row < GRID_ROWS - 1,
        (0, -1): col > 0,
        (0, 1): col < GRID_COLS - 1,
    }
    for dr in (-1, 1):
        for dc in (-1, 1):
            has[dr, dc] = has[dr, 0] & has[0, dc]
    sides = list(has)

    edge = (row == 0) | (row == GRID_ROWS - 1) | (col == 0) | (col == GRID_COLS - 1)

    @pl.when(edge)
    def _():
        stage[...] = jnp.zeros_like(stage)

    barrier = pltpu.get_barrier_semaphore()
    for dr, dc in sides:

        @pl.when(has[dr, dc])
        def _(dr=dr, dc=dc):
            pl.semaphore_signal(
                barrier, inc=1, device_id={"row": row + dr, "col": col + dc}, device_id_type=MESH
            )

    pl.semaphore_signal(barrier, inc=1, device_id={"cfg": 1 - cfg}, device_id_type=MESH)

    own = pltpu.make_async_copy(
        features.at[0], stage.at[pl.ds(HALO, ROWS), pl.ds(STRIP, COLS)], load_sem
    )
    own.start()
    loads = []
    for n in range(4):
        load = pltpu.make_async_copy(weight.at[n // 2, n % 2], wraw.at[n], wsem.at[n])
        load.start()
        loads.append(load)

    groups = lax.broadcasted_iota(jnp.int32, (GROUPS, C), 0)
    channels = lax.broadcasted_iota(jnp.int32, (GROUPS, C), 1)
    lowest = groups * (C // GROUPS)
    spread = jnp.where((channels >= lowest) & (channels < lowest + C // GROUPS), 1.0, 0.0).astype(F32)

    def to_channels(value):
        total = None
        for part in exact_parts(value):
            term = jnp.dot(part, spread, preferred_element_type=F32)
            total = term if total is None else total + term
        return total

    scale = to_channels(lax.rsqrt(var[:, 0, :] + NORM_EPS)) * gain[...]
    offset = shift[...] - to_channels(mean[:, 0, :]) * scale
    params[...] = jnp.zeros_like(params)
    for n in range(5):
        add = offset[n : n + 1]
        if n in (1, 3):
            k = n // 2
            add = add + scale[n : n + 1] * (bias[k, 0:1] + emb[0, k : k + 1])
        params[A_COL + n : A_COL + n + 1, 0:C] = 0.5 * scale[n : n + 1]
        params[B_COL + n : B_COL + n + 1, 0:C] = 0.5 * add
    for k in range(2):
        params[BIAS_COL + k : BIAS_COL + k + 1, 0:C] = bias[k, 1:2]
    turned_params = jnp.transpose(params[...])
    for n in range(12):
        pcols[n] = jnp.broadcast_to(turned_params[0:C, n : n + 1], (C, LANES))

    wout[...] = jnp.zeros_like(wout)
    for t in range(9):
        wout[8 * t : 8 * t + 4, :] = out_weight[t].astype(F32)

    for n in range(5):
        cell = lax.broadcasted_iota(jnp.int32, (8, masks.shape[2]), 1) + n * STEP
        cell_row = lax.shift_right_logical(cell * 28340, 21)
        cell_col = cell - cell_row * WIDE
        grid_row = cell_row + (row * ROWS - HALO)
        grid_col = cell_col + (col * COLS - HALO)
        inside = (
            (grid_row >= 0)
            & (grid_row < GRID_ROWS * ROWS)
            & (grid_col >= 0)
            & (grid_col < GRID_COLS * COLS)
        )
        masks[n] = jnp.where(inside, 1.0, 0.0).astype(F32)

    eye_row = lax.broadcasted_iota(jnp.int32, (C, C), 0)
    eye_col = lax.broadcasted_iota(jnp.int32, (C, C), 1)
    eye = jnp.where(eye_row == eye_col, 1.0, 0.0).astype(BF)

    def flipped(value):
        return lax.dot_general(
            eye, value, (((1,), (1,)), ((), ())), preferred_element_type=F32
        ).astype(BF)

    arrivals = sum(jnp.where(has[s], 1, 0) for s in sides) + 1
    pl.semaphore_wait(barrier, arrivals)

    row_src = {-1: pl.ds(0, HALO), 0: pl.ds(0, ROWS), 1: pl.ds(ROWS - HALO, HALO)}
    row_dst = {-1: pl.ds(HALO + ROWS, HALO), 0: pl.ds(HALO, ROWS), 1: pl.ds(0, HALO)}
    col_src = {-1: pl.ds(0, STRIP), 0: pl.ds(0, COLS), 1: pl.ds(COLS - STRIP, STRIP)}
    col_dst = {-1: pl.ds(STRIP + COLS, STRIP), 0: pl.ds(STRIP, COLS), 1: pl.ds(0, STRIP)}
    copies = {}
    for n, (dr, dc) in enumerate(sides):
        copy = pltpu.make_async_remote_copy(
            src_ref=features.at[0, row_src[dr], col_src[dc]],
            dst_ref=stage.at[row_dst[dr], col_dst[dc]],
            send_sem=send_sem.at[n],
            recv_sem=recv_sem.at[n],
            device_id={"row": row + dr, "col": col + dc},
            device_id_type=MESH,
        )
        copies[dr, dc] = copy

        @pl.when(has[dr, dc])
        def _(copy=copy):
            copy.start()

    for n in range(4):
        loads[n].wait()

        @pl.loop(0, 1)
        def _(_, n=n):
            wflat[n] = flipped(wraw[n].reshape(9 * C, C))

    own.wait()
    for dr, dc in sides:
        copy = copies[dr, dc]

        @pl.when(has[-dr, -dc])
        def _(copy=copy):
            copy.wait_recv()

    def silu(dest, values, norm, frame, first):
        for n in range(values.shape[1] // LANES):
            part = slice(n * LANES, (n + 1) * LANES)
            place = slice(first + n * LANES, first + (n + 1) * LANES)
            half = values[:, part] * pcols[A_COL + norm] + pcols[B_COL + norm]
            masked = half * masks[frame, 0:1, place]
            dest[:, place] = (masked * (1.0 + jnp.tanh(half))).astype(BF)

    for first, count in ((HALO, ROWS), (0, HALO), (HALO + ROWS, HALO)):
        turned = flipped(stage[first : first + count].reshape(count * STAGE, C))
        for n in range(count):
            begin = n * STAGE + STRIP - HALO
            hid_a[:, (first + n) * WIDE : (first + n + 1) * WIDE] = turned[:, begin : begin + WIDE]
    hid_a[:, TALL * WIDE :] = jnp.zeros((C, hid_a.shape[1] - TALL * WIDE), BF)
    for n in range(hid_a.shape[1] // TILE):
        part = slice(n * TILE, (n + 1) * TILE)
        silu(act_a, hid_a[:, part].astype(F32), 0, 0, n * TILE)

    def conv(layer, source, finish):
        size = TILES[layer] * TILE
        for p in range(3):
            for q in range(3):
                tap = 3 * p + q
                patches[tap * C : (tap + 1) * C, 0:size] = source[:, p * WIDE + q : p * WIDE + q + size]
        for n in range(TILES[layer]):
            part = slice(n * TILE, (n + 1) * TILE)
            finish(part, jnp.dot(wflat[layer], patches[:, part], preferred_element_type=F32))

    def inner(layer, dest):
        def finish(part, total):
            silu(dest, total, layer + 1, layer + 1, part.start)

        return finish

    def outer(layer, before, after, dest):
        k = layer // 2

        def finish(part, total):
            for n in range(TILE // LANES):
                place = slice(part.start + n * LANES, part.start + (n + 1) * LANES)
                skip = before[:, place].astype(F32)
                inc = total[:, n * LANES : (n + 1) * LANES] + pcols[BIAS_COL + k]
                hidden = (skip + inc).astype(BF)
                if after is not None:
                    after[:, place] = hidden
                silu(dest, hidden.astype(F32), layer + 1, layer + 1, place.start)

        return finish

    def shifted(dest, source, layer):
        size = TILES[layer] * TILE
        dest[:, 0:size] = source[:, 2 * STEP : 2 * STEP + size]

    shifted(hid_s, hid_a, 1)
    conv(0, act_a, inner(0, act_b))
    conv(1, act_b, outer(1, hid_s, hid_b, act_a))
    conv(2, act_a, inner(2, act_b))
    shifted(hid_s, hid_b, 3)
    conv(3, act_b, outer(3, hid_s, None, act_a))

    size = eps.shape[2]
    taps[...] = jnp.dot(wout[...].astype(BF), act_a[:, 0 : taps.shape[1]], preferred_element_type=F32)
    total = None
    for p in range(3):
        for q in range(3):
            t = 3 * p + q
            begin = p * WIDE + q
            term = taps[8 * t : 8 * t + 8, begin : begin + size]
            total = term if total is None else total + term
    for o in range(4):
        eps[o // 2, o % 2 : o % 2 + 1, :] = total[o : o + 1] + out_bias[o]

    swap = pltpu.make_async_remote_copy(
        src_ref=eps.at[1 - cfg],
        dst_ref=partner,
        send_sem=cfg_send,
        recv_sem=cfg_recv,
        device_id={"cfg": 1 - cfg},
        device_id_type=MESH,
    )
    swap.start()
    for dr, dc in sides:
        copy = copies[dr, dc]

        @pl.when(has[dr, dc])
        def _(copy=copy):
            copy.wait_send()

    swap.wait()
    mine, other = eps[cfg], partner[...]
    uncond = jnp.where(cfg == 1, other, mine)
    cond = jnp.where(cfg == 1, mine, other)
    guided = uncond + guidance[0] * (cond - uncond)
    step = timestep[0]
    c_latent, c_guided = coeffs[0, step], coeffs[1, step]
    for n in range(ROWS):
        out[n] = c_latent * latent[n] + c_guided * guided[:, n * WIDE : n * WIDE + COLS]


def per_device(
    features,
    latent,
    conv_weight,
    conv_bias,
    norm_gain,
    norm_shift,
    emb_shift,
    stale_mean,
    stale_var,
    out_weight,
    out_bias,
    guidance,
    timestep,
    coeffs,
):
    hbm = pl.BlockSpec(memory_space=pl.ANY)
    vmem = pl.BlockSpec(memory_space=pltpu.VMEM)
    smem = pl.BlockSpec(memory_space=pltpu.SMEM)
    dma = pltpu.SemaphoreType.DMA
    lanes = 1792
    def swapped(value):
        return jnp.transpose(value, (1, 0, 2))

    result = pl.pallas_call(
        kernel,
        out_shape=jax.ShapeDtypeStruct((ROWS, 2, COLS), F32),
        in_specs=[hbm, hbm] + [vmem] * 8 + [smem] * 4,
        out_specs=vmem,
        scratch_shapes=[
            pltpu.VMEM((TALL, STAGE, C), BF),
            pltpu.VMEM((4, 9, C, C), BF),
            pltpu.VMEM((4, C, 9 * C), BF),
            pltpu.VMEM((9 * C, TILES[0] * TILE), BF),
            pltpu.VMEM((C, lanes), BF),
            pltpu.VMEM((C, lanes), BF),
            pltpu.VMEM((C, lanes), BF),
            pltpu.VMEM((C, lanes), BF),
            pltpu.VMEM((C, lanes), BF),
            pltpu.VMEM((128, 384), F32),
            pltpu.VMEM((12, C, LANES), F32),
            pltpu.VMEM((5, 8, lanes), F32),
            pltpu.VMEM((72, C), F32),
            pltpu.VMEM((72, 1152), F32),
            pltpu.VMEM((2, 2, 896), F32),
            pltpu.VMEM((2, 896), F32),
            dma,
            dma((4,)),
            dma((8,)),
            dma((8,)),
            dma,
            dma,
        ],
        compiler_params=pltpu.CompilerParams(
            collective_id=0, has_side_effects=True, vmem_limit_bytes=58 * 2**20
        ),
        cost_estimate=pl.CostEstimate(
            flops=12 * 10**9, bytes_accessed=10 * 2**20, transcendentals=2 * 10**6
        ),
    )(
        features,
        conv_weight,
        swapped(latent),
        conv_bias,
        norm_gain,
        norm_shift,
        emb_shift,
        swapped(stale_mean),
        swapped(stale_var),
        jnp.transpose(out_weight, (0, 2, 1)),
        out_bias,
        guidance,
        timestep,
        jnp.transpose(coeffs),
    )
    return swapped(result)


def solution(mesh):
    return jax.shard_map(
        per_device,
        mesh=mesh,
        in_specs=(
            P("cfg", "row", "col", None),
            P("cfg", "row", "col"),
            P(),
            P(),
            P(),
            P(),
            P("cfg", None, None),
            P("cfg", None, None),
            P("cfg", None, None),
            P(),
            P(),
            P(),
            P(),
            P(),
        ),
        out_specs=P("cfg", "row", "col"),
        check_vma=False,
    )
```

```python
import jax
import jax.numpy as jnp
from jax import lax
from jax.experimental import pallas as pl
from jax.experimental.pallas import tpu as pltpu
from jax.sharding import PartitionSpec as P

MESH = pl.DeviceIdType.MESH
BF, F32 = jnp.bfloat16, jnp.float32

C = 320
GROUPS = 32
ROWS, COLS = 12, 64
HALO = 5
WIDE = COLS + 2 * HALO
TALL = ROWS + 2 * HALO
STRIP = 8
LEFT = 16
STAGE = COLS + 2 * LEFT
CORNER = 6 * STRIP
PARTS = (((HALO, ROWS, 0),), ((0, HALO, -1), (HALO + ROWS, HALO, 1)))
STEP = WIDE + 1
TILE = 256
LANES = 128
TILES = (6, 6, 5, 5)
GRID_ROWS, GRID_COLS = 16, 16
NORM_EPS = 1e-05

A_COL, B_COL, BIAS_COL = 0, 5, 10


def exact_parts(value):
    high = value.astype(BF).astype(F32)
    mid = (value - high).astype(BF).astype(F32)
    return high, mid, value - high - mid


def kernel(
    features,
    weight,
    guidance_in,
    timestep_in,
    coeffs_in,
    out_bias_in,
    latent_in,
    bias_in,
    gain_in,
    shift_in,
    emb_in,
    mean_in,
    var_in,
    out_weight_in,
    out,
    stage_own,
    stage_halo,
    strips,
    sides_in,
    corners_in,
    guidance,
    timestep,
    coeffs,
    out_bias,
    latent,
    bias,
    gain,
    shift,
    emb,
    mean,
    var,
    out_weight,
    small_sem,
    wraw,
    wflat,
    patches,
    act_a,
    act_b,
    hid_a,
    hid_b,
    hid_s,
    params,
    pcols,
    masks,
    wout,
    taps,
    eps,
    partner,
    load_sem,
    wsem,
    send_sem,
    recv_sem,
    cfg_send,
    cfg_recv,
):
    row, col, cfg = lax.axis_index("row"), lax.axis_index("col"), lax.axis_index("cfg")
    has = {
        (-1, 0): row > 0,
        (1, 0): row < GRID_ROWS - 1,
        (0, -1): col > 0,
        (0, 1): col < GRID_COLS - 1,
    }
    for dr in (-1, 1):
        for dc in (-1, 1):
            has[dr, dc] = has[dr, 0] & has[0, dc]
    sides = list(has)

    edge = (row == 0) | (row == GRID_ROWS - 1) | (col == 0) | (col == GRID_COLS - 1)

    @pl.when(edge)
    def _():
        for ref in (stage_halo, sides_in, corners_in):
            ref[...] = jnp.zeros_like(ref)

    barrier = pltpu.get_barrier_semaphore()
    for dr, dc in sides:

        @pl.when(has[dr, dc])
        def _(dr=dr, dc=dc):
            pl.semaphore_signal(
                barrier, inc=1, device_id={"row": row + dr, "col": col + dc}, device_id_type=MESH
            )

    pl.semaphore_signal(barrier, inc=1, device_id={"cfg": 1 - cfg}, device_id_type=MESH)

    own = pltpu.make_async_copy(
        features.at[0], stage_own.at[:, pl.ds(LEFT, COLS)], load_sem
    )
    own.start()
    small = []
    for n, (source, dest) in enumerate(
        (
            (gain_in, gain),
            (shift_in, shift),
            (mean_in, mean),
            (var_in, var),
            (bias_in, bias),
            (emb_in, emb),
            (out_weight_in, out_weight),
            (latent_in, latent),
            (guidance_in, guidance),
            (timestep_in, timestep),
            (coeffs_in, coeffs),
            (out_bias_in, out_bias),
        )
    ):
        load = pltpu.make_async_copy(source, dest, small_sem.at[n])
        load.start()
        small.append(load)
    early, small = small[:7], small[7:]
    loads = []
    for n in range(4):
        load = pltpu.make_async_copy(weight.at[n // 2, n % 2], wraw.at[n], wsem.at[n])
        load.start()
        loads.append(load)

    for load in early:
        load.wait()
    groups = lax.broadcasted_iota(jnp.int32, (GROUPS, C), 0)
    channels = lax.broadcasted_iota(jnp.int32, (GROUPS, C), 1)
    lowest = groups * (C // GROUPS)
    spread = jnp.where((channels >= lowest) & (channels < lowest + C // GROUPS), 1.0, 0.0).astype(F32)

    def to_channels(value):
        total = None
        for part in exact_parts(value):
            term = jnp.dot(part, spread, preferred_element_type=F32)
            total = term if total is None else total + term
        return total

    scale = to_channels(lax.rsqrt(var[:, 0, :] + NORM_EPS)) * gain[...]
    offset = shift[...] - to_channels(mean[:, 0, :]) * scale
    params[...] = jnp.zeros_like(params)
    for n in range(5):
        add = offset[n : n + 1]
        if n in (1, 3):
            k = n // 2
            add = add + scale[n : n + 1] * (bias[k, 0:1] + emb[0, k : k + 1])
        params[A_COL + n : A_COL + n + 1, 0:C] = 0.5 * scale[n : n + 1]
        params[B_COL + n : B_COL + n + 1, 0:C] = 0.5 * add
    for k in range(2):
        params[BIAS_COL + k : BIAS_COL + k + 1, 0:C] = bias[k, 1:2]
    turned_params = jnp.transpose(params[...])
    for n in range(12):
        pcols[n] = jnp.broadcast_to(turned_params[0:C, n : n + 1], (C, LANES))

    wout[...] = jnp.zeros_like(wout)
    for t in range(9):
        wout[8 * t : 8 * t + 4, :] = out_weight[t].astype(F32)

    for n in range(5):
        cell = lax.broadcasted_iota(jnp.int32, (8, masks.shape[2]), 1) + n * STEP
        cell_row = lax.shift_right_logical(cell * 28340, 21)
        cell_col = cell - cell_row * WIDE
        grid_row = cell_row + (row * ROWS - HALO)
        grid_col = cell_col + (col * COLS - HALO)
        inside = (
            (grid_row >= 0)
            & (grid_row < GRID_ROWS * ROWS)
            & (grid_col >= 0)
            & (grid_col < GRID_COLS * COLS)
        )
        masks[n] = jnp.where(inside, 1.0, 0.0).astype(F32)

    eye_row = lax.broadcasted_iota(jnp.int32, (C, C), 0)
    eye_col = lax.broadcasted_iota(jnp.int32, (C, C), 1)
    eye = jnp.where(eye_row == eye_col, 1.0, 0.0).astype(BF)

    def flipped(value):
        return lax.dot_general(
            eye, value, (((1,), (1,)), ((), ())), preferred_element_type=F32
        ).astype(BF)

    own.wait()
    for n in range(ROWS):
        cells = slice(n * STRIP, (n + 1) * STRIP)
        strips[0, cells] = stage_own[n, LEFT : LEFT + STRIP]
        strips[1, cells] = stage_own[n, LEFT + COLS - STRIP : LEFT + COLS]

    arrivals = sum(jnp.where(has[s], 1, 0) for s in sides) + 1
    pl.semaphore_wait(barrier, arrivals)

    copies = []

    def send(dr, dc, source, dest):
        n = len(copies)
        copy = pltpu.make_async_remote_copy(
            src_ref=source,
            dst_ref=dest,
            send_sem=send_sem.at[n],
            recv_sem=recv_sem.at[n],
            device_id={"row": row + dr, "col": col + dc},
            device_id_type=MESH,
        )
        copies.append((copy, has[dr, dc], has[-dr, -dc]))

        @pl.when(has[dr, dc])
        def _():
            copy.start()

        return n

    def arrived(n):
        copy, _, comes = copies[n]

        @pl.when(comes)
        def _():
            copy.wait_recv()

    waits = ([], [])
    for dc in (-1, 1):
        waits[0].append(send(0, dc, strips.at[(1 + dc) // 2], sides_in.at[(1 - dc) // 2]))
    for dr in (-1, 1):
        for dc in (-1, 1):
            cells = pl.ds(0, CORNER) if dr < 0 else pl.ds(ROWS * STRIP - CORNER, CORNER)
            n = send(
                dr,
                dc,
                strips.at[(1 + dc) // 2, cells],
                corners_in.at[(1 - dr) // 2, (1 - dc) // 2],
            )
            waits[1].append(n)
    for dr in (-1, 1):
        begin = 0 if dr < 0 else ROWS - HALO
        n = send(
            dr,
            0,
            features.at[0, pl.ds(begin, HALO)],
            stage_halo.at[pl.ds(HALO if dr < 0 else 0, HALO), pl.ds(LEFT, COLS)],
        )
        waits[1].append(n)

    for n in range(4):
        loads[n].wait()

        @pl.loop(0, 1)
        def _(_, n=n):
            wflat[n] = flipped(wraw[n].reshape(9 * C, C))

    def silu(dest, values, norm, frame, first):
        for n in range(values.shape[1] // LANES):
            part = slice(n * LANES, (n + 1) * LANES)
            place = slice(first + n * LANES, first + (n + 1) * LANES)
            half = values[:, part] * pcols[A_COL + norm] + pcols[B_COL + norm]
            masked = half * masks[frame, 0:1, place]
            dest[:, place] = (masked * (1.0 + jnp.tanh(half))).astype(BF)

    def take(part):
        for n in waits[part]:
            arrived(n)
        ref = (stage_own, stage_halo)[part]
        places = []
        for first, count, side in PARTS[part]:
            for n in range(count):
                at = len(places)
                for half, place in ((0, LEFT - STRIP), (1, LEFT + COLS)):
                    if side == 0:
                        cells = sides_in[half, n * STRIP : (n + 1) * STRIP]
                    else:
                        r = n + 1 if side < 0 else n
                        cells = corners_in[(1 + side) // 2, half, r * STRIP : (r + 1) * STRIP]
                    ref[at, place : place + STRIP] = cells
                places.append(first + n)
        turned = flipped(ref[...].reshape(len(places) * STAGE, C))
        for at, n in enumerate(places):
            begin = at * STAGE + LEFT - HALO
            hid_a[:, n * WIDE : (n + 1) * WIDE] = turned[:, begin : begin + WIDE]

    def first_act(begin, end):
        silu(act_a, hid_a[:, begin:end].astype(F32), 0, 0, begin)

    def gather(source, begin, end):
        for p in range(3):
            for q in range(3):
                tap = 3 * p + q
                shift_by = p * WIDE + q
                patches[tap * C : (tap + 1) * C, begin:end] = source[:, begin + shift_by : end + shift_by]

    def product(layer, n, finish):
        part = slice(n * TILE, (n + 1) * TILE)
        finish(part, jnp.dot(wflat[layer], patches[:, part], preferred_element_type=F32))

    def conv(layer, source, finish):
        gather(source, 0, TILES[layer] * TILE)
        for n in range(TILES[layer]):
            product(layer, n, finish)

    def inner(layer, dest):
        def finish(part, total):
            silu(dest, total, layer + 1, layer + 1, part.start)

        return finish

    def outer(layer, before, after, dest):
        k = layer // 2

        def finish(part, total):
            for n in range(TILE // LANES):
                place = slice(part.start + n * LANES, part.start + (n + 1) * LANES)
                skip = before[:, place].astype(F32)
                inc = total[:, n * LANES : (n + 1) * LANES] + pcols[BIAS_COL + k]
                hidden = (skip + inc).astype(BF)
                if after is not None:
                    after[:, place] = hidden
                silu(dest, hidden.astype(F32), layer + 1, layer + 1, place.start)

        return finish

    def shifted(dest, source, layer):
        size = TILES[layer] * TILE
        dest[:, 0:size] = source[:, 2 * STEP : 2 * STEP + size]

    hid_a[:, TALL * WIDE :] = jnp.zeros((C, hid_a.shape[1] - TALL * WIDE), BF)
    finish = inner(0, act_b)
    take(0)
    first_act(384, 1280)
    gather(act_a, 512, 1024)
    product(0, 2, finish)
    product(0, 3, finish)
    take(1)
    first_act(0, 384)
    first_act(1152, 1792)
    gather(act_a, 0, 512)
    gather(act_a, 1024, 1536)
    for n in (0, 1, 4, 5):
        product(0, n, finish)
    shifted(hid_s, hid_a, 1)
    conv(1, act_b, outer(1, hid_s, hid_b, act_a))
    conv(2, act_a, inner(2, act_b))
    shifted(hid_s, hid_b, 3)
    conv(3, act_b, outer(3, hid_s, None, act_a))

    for load in small:
        load.wait()
    size = eps.shape[2]
    taps[...] = jnp.dot(wout[...].astype(BF), act_a[:, 0 : taps.shape[1]], preferred_element_type=F32)
    total = None
    for p in range(3):
        for q in range(3):
            t = 3 * p + q
            begin = p * WIDE + q
            term = taps[8 * t : 8 * t + 8, begin : begin + size]
            total = term if total is None else total + term
    for o in range(4):
        eps[o // 2, o % 2 : o % 2 + 1, :] = total[o : o + 1] + out_bias[o]

    swap = pltpu.make_async_remote_copy(
        src_ref=eps.at[1 - cfg],
        dst_ref=partner,
        send_sem=cfg_send,
        recv_sem=cfg_recv,
        device_id={"cfg": 1 - cfg},
        device_id_type=MESH,
    )
    swap.start()
    for copy, goes, _ in copies:

        @pl.when(goes)
        def _(copy=copy):
            copy.wait_send()

    swap.wait()
    mine, other = eps[cfg], partner[...]
    uncond = jnp.where(cfg == 1, other, mine)
    cond = jnp.where(cfg == 1, mine, other)
    guided = uncond + guidance[0] * (cond - uncond)
    step = timestep[0]
    c_latent, c_guided = coeffs[0, step], coeffs[1, step]
    for n in range(ROWS):
        out[n] = c_latent * latent[n] + c_guided * guided[:, n * WIDE : n * WIDE + COLS]


def per_device(
    features,
    latent,
    conv_weight,
    conv_bias,
    norm_gain,
    norm_shift,
    emb_shift,
    stale_mean,
    stale_var,
    out_weight,
    out_bias,
    guidance,
    timestep,
    coeffs,
):
    hbm = pl.BlockSpec(memory_space=pl.ANY)
    vmem = pl.BlockSpec(memory_space=pltpu.VMEM)
    dma = pltpu.SemaphoreType.DMA
    lanes = 1792
    def swapped(value):
        return jnp.transpose(value, (1, 0, 2))

    result = pl.pallas_call(
        kernel,
        out_shape=pltpu.VMEM((ROWS, 2, COLS), F32),
        in_specs=[hbm] * 14,
        out_specs=vmem,
        scratch_shapes=[
            pltpu.VMEM((ROWS, STAGE, C), BF),
            pltpu.VMEM((2 * HALO, STAGE, C), BF),
            pltpu.VMEM((2, ROWS * STRIP, C), BF),
            pltpu.VMEM((2, ROWS * STRIP, C), BF),
            pltpu.VMEM((2, 2, CORNER, C), BF),
            pltpu.SMEM((1,), F32),
            pltpu.SMEM((1,), jnp.int32),
            pltpu.SMEM((2, 50), F32),
            pltpu.SMEM((4,), F32),
            pltpu.VMEM((ROWS, 2, COLS), F32),
            pltpu.VMEM((2, 2, C), F32),
            pltpu.VMEM((5, C), F32),
            pltpu.VMEM((5, C), F32),
            pltpu.VMEM((1, 2, C), F32),
            pltpu.VMEM((5, 1, GROUPS), F32),
            pltpu.VMEM((5, 1, GROUPS), F32),
            pltpu.VMEM((9, 4, C), BF),
            dma((12,)),
            pltpu.VMEM((4, 9, C, C), BF),
            pltpu.VMEM((4, C, 9 * C), BF),
            pltpu.VMEM((9 * C, TILES[0] * TILE), BF),
            pltpu.VMEM((C, lanes), BF),
            pltpu.VMEM((C, lanes), BF),
            pltpu.VMEM((C, lanes), BF),
            pltpu.VMEM((C, lanes), BF),
            pltpu.VMEM((C, lanes), BF),
            pltpu.VMEM((128, 384), F32),
            pltpu.VMEM((12, C, LANES), F32),
            pltpu.VMEM((5, 8, lanes), F32),
            pltpu.VMEM((72, C), F32),
            pltpu.VMEM((72, 1152), F32),
            pltpu.VMEM((2, 2, 896), F32),
            pltpu.VMEM((2, 896), F32),
            dma,
            dma((4,)),
            dma((8,)),
            dma((8,)),
            dma,
            dma,
        ],
        compiler_params=pltpu.CompilerParams(
            collective_id=0, has_side_effects=True, vmem_limit_bytes=58 * 2**20
        ),
        cost_estimate=pl.CostEstimate(
            flops=12 * 10**9, bytes_accessed=10 * 2**20, transcendentals=2 * 10**6
        ),
    )(
        features,
        conv_weight,
        guidance,
        timestep,
        jnp.transpose(coeffs),
        out_bias,
        swapped(latent),
        conv_bias,
        norm_gain,
        norm_shift,
        emb_shift,
        swapped(stale_mean),
        swapped(stale_var),
        jnp.transpose(out_weight, (0, 2, 1)),
    )
    return swapped(result)


def solution(mesh):
    return jax.shard_map(
        per_device,
        mesh=mesh,
        in_specs=(
            P("cfg", "row", "col", None),
            P("cfg", "row", "col"),
            P(),
            P(),
            P(),
            P(),
            P("cfg", None, None),
            P("cfg", None, None),
            P("cfg", None, None),
            P(),
            P(),
            P(),
            P(),
            P(),
        ),
        out_specs=P("cfg", "row", "col"),
        check_vma=False,
    )
```

```python
import jax
import jax.numpy as jnp
from jax import lax
from jax.experimental import pallas as pl
from jax.experimental.pallas import tpu as pltpu
from jax.sharding import PartitionSpec as P

MESH = pl.DeviceIdType.MESH
BF, F32 = jnp.bfloat16, jnp.float32

C = 320
GROUPS = 32
ROWS, COLS = 12, 64
HALO = 5
WIDE = COLS + 2 * HALO
TALL = ROWS + 2 * HALO
STRIP = 8
LEFT = 16
STAGE = COLS + 2 * LEFT
CORNER = 6 * STRIP
PARTS = (((HALO, ROWS, 0),), ((0, HALO, -1), (HALO + ROWS, HALO, 1)))
STEP = WIDE + 1
TILE = 256
LANES = 128
SIZES = (1536, 1408, 1280, 1152)
GRID_ROWS, GRID_COLS = 16, 16
NORM_EPS = 1e-05
MAIN, REST = 256, 64

A_COL, B_COL, BIAS_COL = 0, 5, 10


def exact_parts(value):
    high = value.astype(BF).astype(F32)
    mid = (value - high).astype(BF).astype(F32)
    return high, mid, value - high - mid


def kernel(
    features,
    weight,
    guidance_in,
    timestep_in,
    coeffs_in,
    out_bias_in,
    latent_in,
    bias_in,
    gain_in,
    shift_in,
    emb_in,
    mean_in,
    var_in,
    out_weight_in,
    out,
    stage_own,
    stage_halo,
    strips,
    sides_in,
    corners_in,
    rest_out,
    rest_in,
    guidance,
    timestep,
    coeffs,
    out_bias,
    latent,
    bias,
    gain,
    shift,
    emb,
    mean,
    var,
    out_weight,
    small_sem,
    wraw,
    wflat,
    patches,
    act_a,
    act_b,
    hid_a,
    hid_b,
    hid_s,
    params,
    pcols,
    masks,
    wout,
    taps,
    eps,
    partner,
    load_sem,
    wsem,
    send_sem,
    recv_sem,
    cfg_send,
    cfg_recv,
):
    row, col, cfg = lax.axis_index("row"), lax.axis_index("col"), lax.axis_index("cfg")
    has = {
        (-1, 0): row > 0,
        (1, 0): row < GRID_ROWS - 1,
        (0, -1): col > 0,
        (0, 1): col < GRID_COLS - 1,
    }
    for dr in (-1, 1):
        for dc in (-1, 1):
            has[dr, dc] = has[dr, 0] & has[0, dc]
    sides = list(has)

    edge = (row == 0) | (row == GRID_ROWS - 1) | (col == 0) | (col == GRID_COLS - 1)

    @pl.when(edge)
    def _():
        for ref in (stage_halo, sides_in, corners_in, rest_in):
            ref[...] = jnp.zeros_like(ref)

    barrier = pltpu.get_barrier_semaphore()
    for dr, dc in sides:

        @pl.when(has[dr, dc])
        def _(dr=dr, dc=dc):
            pl.semaphore_signal(
                barrier, inc=1, device_id={"row": row + dr, "col": col + dc}, device_id_type=MESH
            )

    pl.semaphore_signal(barrier, inc=1, device_id={"cfg": 1 - cfg}, device_id_type=MESH)

    own = pltpu.make_async_copy(
        features.at[0], stage_own.at[:, pl.ds(LEFT, COLS)], load_sem
    )
    own.start()
    small = []
    for n, (source, dest) in enumerate(
        (
            (gain_in, gain),
            (shift_in, shift),
            (mean_in, mean),
            (var_in, var),
            (bias_in, bias),
            (emb_in, emb),
            (out_weight_in, out_weight),
            (latent_in, latent),
            (guidance_in, guidance),
            (timestep_in, timestep),
            (coeffs_in, coeffs),
            (out_bias_in, out_bias),
        )
    ):
        load = pltpu.make_async_copy(source, dest, small_sem.at[n])
        load.start()
        small.append(load)
    early, small = small[:7], small[7:]
    loads = []
    for n in range(4):
        load = pltpu.make_async_copy(weight.at[n // 2, n % 2], wraw.at[n], wsem.at[n])
        load.start()
        loads.append(load)

    own.wait()
    for n in range(ROWS):
        cells = slice(n * STRIP, (n + 1) * STRIP)
        strips[0, cells] = stage_own[n, LEFT : LEFT + STRIP]
        strips[1, cells] = stage_own[n, LEFT + COLS - STRIP : LEFT + COLS]
    for n in range(HALO):
        for side in range(2):
            r = n + side * (ROWS - HALO)
            for half in range(2):
                begin = LEFT + half * COLS // 2
                rest_out[side, n, :, half * REST : (half + 1) * REST] = stage_own[
                    r, begin : begin + COLS // 2, MAIN:C
                ]

    arrivals = sum(jnp.where(has[s], 1, 0) for s in sides) + 1
    pl.semaphore_wait(barrier, arrivals)

    copies = []

    def send(dr, dc, source, dest):
        n = len(copies)
        copy = pltpu.make_async_remote_copy(
            src_ref=source,
            dst_ref=dest,
            send_sem=send_sem.at[n],
            recv_sem=recv_sem.at[n],
            device_id={"row": row + dr, "col": col + dc},
            device_id_type=MESH,
        )
        copies.append((copy, has[dr, dc], has[-dr, -dc]))

        @pl.when(has[dr, dc])
        def _():
            copy.start()

        return n

    def arrived(n):
        copy, _, comes = copies[n]

        @pl.when(comes)
        def _():
            copy.wait_recv()

    waits = ([], [])
    for dc in (-1, 1):
        waits[0].append(send(0, dc, strips.at[(1 + dc) // 2], sides_in.at[(1 - dc) // 2]))
    for dr in (-1, 1):
        for dc in (-1, 1):
            cells = pl.ds(0, CORNER) if dr < 0 else pl.ds(ROWS * STRIP - CORNER, CORNER)
            n = send(
                dr,
                dc,
                strips.at[(1 + dc) // 2, cells],
                corners_in.at[(1 - dr) // 2, (1 - dc) // 2],
            )
            waits[1].append(n)
    for dr in (-1, 1):
        n = send(dr, 0, rest_out.at[(1 + dr) // 2], rest_in.at[(1 - dr) // 2])
        waits[1].append(n)
    for dr in (-1, 1):
        begin = 0 if dr < 0 else ROWS - HALO
        n = send(
            dr,
            0,
            features.at[0, pl.ds(begin, HALO), :, pl.ds(0, MAIN)],
            stage_halo.at[pl.ds(HALO if dr < 0 else 0, HALO), pl.ds(LEFT, COLS), pl.ds(0, MAIN)],
        )
        waits[1].append(n)

    for load in early:
        load.wait()
    groups = lax.broadcasted_iota(jnp.int32, (GROUPS, C), 0)
    channels = lax.broadcasted_iota(jnp.int32, (GROUPS, C), 1)
    lowest = groups * (C // GROUPS)
    spread = jnp.where((channels >= lowest) & (channels < lowest + C // GROUPS), 1.0, 0.0).astype(F32)

    def to_channels(value):
        total = None
        for part in exact_parts(value):
            term = jnp.dot(part, spread, preferred_element_type=F32)
            total = term if total is None else total + term
        return total

    scale = to_channels(lax.rsqrt(var[:, 0, :] + NORM_EPS)) * gain[...]
    offset = shift[...] - to_channels(mean[:, 0, :]) * scale
    params[...] = jnp.zeros_like(params)
    for n in range(5):
        add = offset[n : n + 1]
        if n in (1, 3):
            k = n // 2
            add = add + scale[n : n + 1] * (bias[k, 0:1] + emb[0, k : k + 1])
        params[A_COL + n : A_COL + n + 1, 0:C] = 0.5 * scale[n : n + 1]
        params[B_COL + n : B_COL + n + 1, 0:C] = 0.5 * add
    for k in range(2):
        params[BIAS_COL + k : BIAS_COL + k + 1, 0:C] = bias[k, 1:2]
    turned_params = jnp.transpose(params[...])
    for n in range(12):
        pcols[n] = jnp.broadcast_to(turned_params[0:C, n : n + 1], (C, LANES))

    wout[...] = jnp.zeros_like(wout)
    for t in range(9):
        wout[8 * t : 8 * t + 4, :] = out_weight[t].astype(F32)

    for n in range(5):
        cell = lax.broadcasted_iota(jnp.int32, (8, masks.shape[2]), 1) + n * STEP
        cell_row = lax.shift_right_logical(cell * 28340, 21)
        cell_col = cell - cell_row * WIDE
        grid_row = cell_row + (row * ROWS - HALO)
        grid_col = cell_col + (col * COLS - HALO)
        inside = (
            (grid_row >= 0)
            & (grid_row < GRID_ROWS * ROWS)
            & (grid_col >= 0)
            & (grid_col < GRID_COLS * COLS)
        )
        masks[n] = jnp.where(inside, 1.0, 0.0).astype(F32)

    eye_row = lax.broadcasted_iota(jnp.int32, (C, C), 0)
    eye_col = lax.broadcasted_iota(jnp.int32, (C, C), 1)
    eye = jnp.where(eye_row == eye_col, 1.0, 0.0).astype(BF)

    def flipped(value):
        return lax.dot_general(
            eye, value, (((1,), (1,)), ((), ())), preferred_element_type=F32
        ).astype(BF)

    for n in range(4):
        loads[n].wait()

        @pl.loop(0, 1)
        def _(_, n=n):
            wflat[n] = flipped(wraw[n].reshape(9 * C, C))

    def silu(dest, values, norm, frame, first):
        for n in range(values.shape[1] // LANES):
            part = slice(n * LANES, (n + 1) * LANES)
            place = slice(first + n * LANES, first + (n + 1) * LANES)
            half = values[:, part] * pcols[A_COL + norm] + pcols[B_COL + norm]
            masked = half * masks[frame, 0:1, place]
            dest[:, place] = (masked * (1.0 + jnp.tanh(half))).astype(BF)

    def take(part):
        for n in waits[part]:
            arrived(n)
        ref = (stage_own, stage_halo)[part]
        places = []
        for first, count, side in PARTS[part]:
            for n in range(count):
                at = len(places)
                for half, place in ((0, LEFT - STRIP), (1, LEFT + COLS)):
                    if side == 0:
                        cells = sides_in[half, n * STRIP : (n + 1) * STRIP]
                    else:
                        r = n + 1 if side < 0 else n
                        cells = corners_in[(1 + side) // 2, half, r * STRIP : (r + 1) * STRIP]
                    ref[at, place : place + STRIP] = cells
                for half in range(2 if side else 0):
                    begin = LEFT + half * COLS // 2
                    ref[at, begin : begin + COLS // 2, MAIN:C] = rest_in[
                        (1 + side) // 2, n, :, half * REST : (half + 1) * REST
                    ]
                places.append(first + n)
        turned = flipped(ref[...].reshape(len(places) * STAGE, C))
        for at, n in enumerate(places):
            begin = at * STAGE + LEFT - HALO
            hid_a[:, n * WIDE : (n + 1) * WIDE] = turned[:, begin : begin + WIDE]

    def first_act(begin, end):
        silu(act_a, hid_a[:, begin:end].astype(F32), 0, 0, begin)

    def gather(source, begin, end):
        for p in range(3):
            for q in range(3):
                tap = 3 * p + q
                shift_by = p * WIDE + q
                wide = end - begin + -(-shift_by // LANES) * LANES
                cells = source[:, begin : begin + wide]
                if shift_by:
                    cells = pltpu.roll(cells, wide - shift_by, 1)
                patches[tap * C : (tap + 1) * C, begin:end] = cells[:, 0 : end - begin]

    def product(layer, n, finish):
        part = slice(n * TILE, min((n + 1) * TILE, SIZES[layer]))
        finish(part, jnp.dot(wflat[layer], patches[:, part], preferred_element_type=F32))

    def conv(layer, source, finish):
        gather(source, 0, SIZES[layer])
        for n in range(-(-SIZES[layer] // TILE)):
            product(layer, n, finish)

    def inner(layer, dest):
        def finish(part, total):
            silu(dest, total, layer + 1, layer + 1, part.start)

        return finish

    def outer(layer, before, after, dest):
        k = layer // 2

        def finish(part, total):
            for n in range(total.shape[1] // LANES):
                place = slice(part.start + n * LANES, part.start + (n + 1) * LANES)
                skip = before[:, place].astype(F32)
                inc = total[:, n * LANES : (n + 1) * LANES] + pcols[BIAS_COL + k]
                hidden = (skip + inc).astype(BF)
                if after is not None:
                    after[:, place] = hidden
                silu(dest, hidden.astype(F32), layer + 1, layer + 1, place.start)

        return finish

    def shifted(dest, source, layer):
        size = SIZES[layer]
        dest[:, 0:size] = source[:, 2 * STEP : 2 * STEP + size]

    hid_a[:, TALL * WIDE :] = jnp.zeros((C, hid_a.shape[1] - TALL * WIDE), BF)
    finish = inner(0, act_b)
    take(0)
    first_act(384, 1280)
    gather(act_a, 512, 1024)
    product(0, 2, finish)
    product(0, 3, finish)
    take(1)
    first_act(0, 384)
    first_act(1152, 1792)
    gather(act_a, 0, 512)
    gather(act_a, 1024, 1536)
    for n in (0, 1, 4, 5):
        product(0, n, finish)
    shifted(hid_s, hid_a, 1)
    conv(1, act_b, outer(1, hid_s, hid_b, act_a))
    conv(2, act_a, inner(2, act_b))
    shifted(hid_s, hid_b, 3)
    conv(3, act_b, outer(3, hid_s, None, act_a))

    for load in small:
        load.wait()
    size = eps.shape[2]
    taps[...] = jnp.dot(wout[...].astype(BF), act_a[:, 0 : taps.shape[1]], preferred_element_type=F32)
    total = None
    for p in range(3):
        for q in range(3):
            t = 3 * p + q
            begin = p * WIDE + q
            term = taps[8 * t : 8 * t + 8, begin : begin + size]
            total = term if total is None else total + term
    for o in range(4):
        eps[o // 2, o % 2 : o % 2 + 1, :] = total[o : o + 1] + out_bias[o]

    swap = pltpu.make_async_remote_copy(
        src_ref=eps.at[1 - cfg],
        dst_ref=partner,
        send_sem=cfg_send,
        recv_sem=cfg_recv,
        device_id={"cfg": 1 - cfg},
        device_id_type=MESH,
    )
    swap.start()
    for copy, goes, _ in copies:

        @pl.when(goes)
        def _(copy=copy):
            copy.wait_send()

    swap.wait()
    mine, other = eps[cfg], partner[...]
    uncond = jnp.where(cfg == 1, other, mine)
    cond = jnp.where(cfg == 1, mine, other)
    guided = uncond + guidance[0] * (cond - uncond)
    step = timestep[0]
    c_latent, c_guided = coeffs[0, step], coeffs[1, step]
    for n in range(ROWS):
        out[n] = c_latent * latent[n] + c_guided * guided[:, n * WIDE : n * WIDE + COLS]


def per_device(
    features,
    latent,
    conv_weight,
    conv_bias,
    norm_gain,
    norm_shift,
    emb_shift,
    stale_mean,
    stale_var,
    out_weight,
    out_bias,
    guidance,
    timestep,
    coeffs,
):
    hbm = pl.BlockSpec(memory_space=pl.ANY)
    vmem = pl.BlockSpec(memory_space=pltpu.VMEM)
    dma = pltpu.SemaphoreType.DMA
    lanes = 1792
    def swapped(value):
        return jnp.transpose(value, (1, 0, 2))

    result = pl.pallas_call(
        kernel,
        out_shape=pltpu.VMEM((ROWS, 2, COLS), F32),
        in_specs=[hbm] * 14,
        out_specs=vmem,
        scratch_shapes=[
            pltpu.VMEM((ROWS, STAGE, C), BF),
            pltpu.VMEM((2 * HALO, STAGE, C), BF),
            pltpu.VMEM((2, ROWS * STRIP, C), BF),
            pltpu.VMEM((2, ROWS * STRIP, C), BF),
            pltpu.VMEM((2, 2, CORNER, C), BF),
            pltpu.VMEM((2, HALO, COLS // 2, 2 * REST), BF),
            pltpu.VMEM((2, HALO, COLS // 2, 2 * REST), BF),
            pltpu.SMEM((1,), F32),
            pltpu.SMEM((1,), jnp.int32),
            pltpu.SMEM((2, 50), F32),
            pltpu.SMEM((4,), F32),
            pltpu.VMEM((ROWS, 2, COLS), F32),
            pltpu.VMEM((2, 2, C), F32),
            pltpu.VMEM((5, C), F32),
            pltpu.VMEM((5, C), F32),
            pltpu.VMEM((1, 2, C), F32),
            pltpu.VMEM((5, 1, GROUPS), F32),
            pltpu.VMEM((5, 1, GROUPS), F32),
            pltpu.VMEM((9, 4, C), BF),
            dma((12,)),
            pltpu.VMEM((4, 9, C, C), BF),
            pltpu.VMEM((4, C, 9 * C), BF),
            pltpu.VMEM((9 * C, SIZES[0]), BF),
            pltpu.VMEM((C, lanes), BF),
            pltpu.VMEM((C, lanes), BF),
            pltpu.VMEM((C, lanes), BF),
            pltpu.VMEM((C, lanes), BF),
            pltpu.VMEM((C, lanes), BF),
            pltpu.VMEM((128, 384), F32),
            pltpu.VMEM((12, C, LANES), F32),
            pltpu.VMEM((5, 8, lanes), F32),
            pltpu.VMEM((72, C), F32),
            pltpu.VMEM((72, 1152), F32),
            pltpu.VMEM((2, 2, 896), F32),
            pltpu.VMEM((2, 896), F32),
            dma,
            dma((4,)),
            dma((10,)),
            dma((10,)),
            dma,
            dma,
        ],
        compiler_params=pltpu.CompilerParams(
            collective_id=0, has_side_effects=True, vmem_limit_bytes=58 * 2**20
        ),
        cost_estimate=pl.CostEstimate(
            flops=12 * 10**9, bytes_accessed=10 * 2**20, transcendentals=2 * 10**6
        ),
    )(
        features,
        conv_weight,
        guidance,
        timestep,
        jnp.transpose(coeffs),
        out_bias,
        swapped(latent),
        conv_bias,
        norm_gain,
        norm_shift,
        emb_shift,
        swapped(stale_mean),
        swapped(stale_var),
        jnp.transpose(out_weight, (0, 2, 1)),
    )
    return swapped(result)


def solution(mesh):
    return jax.shard_map(
        per_device,
        mesh=mesh,
        in_specs=(
            P("cfg", "row", "col", None),
            P("cfg", "row", "col"),
            P(),
            P(),
            P(),
            P(),
            P("cfg", None, None),
            P("cfg", None, None),
            P("cfg", None, None),
            P(),
            P(),
            P(),
            P(),
            P(),
        ),
        out_specs=P("cfg", "row", "col"),
        check_vma=False,
    )
```

```python
import jax
import jax.numpy as jnp
from jax import lax
from jax.experimental import pallas as pl
from jax.experimental.pallas import tpu as pltpu
from jax.sharding import PartitionSpec as P

MESH = pl.DeviceIdType.MESH
BF, F32 = jnp.bfloat16, jnp.float32

C = 320
GROUPS = 32
ROWS, COLS = 12, 64
HALO = 5
WIDE = COLS + 2 * HALO
TALL = ROWS + 2 * HALO
STRIP = 8
LEFT = 16
STAGE = COLS + 2 * LEFT
CORNER = 6 * STRIP
NEAR = (2, 3)
PARTS = (
    ((HALO, ROWS, 0),),
    ((HALO - NEAR[0], NEAR[0], -1), (HALO + ROWS, NEAR[1], 1)),
    ((0, HALO - NEAR[0], -1), (HALO + ROWS + NEAR[1], HALO - NEAR[1], 1)),
)
STEP = WIDE + 1
TILE = 256
LANES = 128
SIZES = (1536, 1408, 1280, 1152)
GRID_ROWS, GRID_COLS = 16, 16
NORM_EPS = 1e-05
MAIN, REST = 256, 64

A_COL, B_COL, BIAS_COL = 0, 5, 10


def exact_parts(value):
    high = value.astype(BF).astype(F32)
    mid = (value - high).astype(BF).astype(F32)
    return high, mid, value - high - mid


def kernel(
    features,
    weight,
    guidance_in,
    timestep_in,
    coeffs_in,
    out_bias_in,
    latent_in,
    bias_in,
    gain_in,
    shift_in,
    emb_in,
    mean_in,
    var_in,
    out_weight_in,
    out,
    stage_own,
    stage_near,
    stage_far,
    strips,
    sides_in,
    corners_in,
    rest_out,
    rest_in,
    guidance,
    timestep,
    coeffs,
    out_bias,
    latent,
    bias,
    gain,
    shift,
    emb,
    mean,
    var,
    out_weight,
    small_sem,
    wraw,
    wflat,
    patches,
    act_a,
    act_b,
    hid_a,
    hid_b,
    hid_s,
    params,
    pcols,
    masks,
    wout,
    taps,
    eps,
    partner,
    load_sem,
    wsem,
    send_sem,
    recv_sem,
    cfg_send,
    cfg_recv,
):
    row, col, cfg = lax.axis_index("row"), lax.axis_index("col"), lax.axis_index("cfg")
    has = {
        (-1, 0): row > 0,
        (1, 0): row < GRID_ROWS - 1,
        (0, -1): col > 0,
        (0, 1): col < GRID_COLS - 1,
    }
    for dr in (-1, 1):
        for dc in (-1, 1):
            has[dr, dc] = has[dr, 0] & has[0, dc]
    sides = list(has)

    edge = (row == 0) | (row == GRID_ROWS - 1) | (col == 0) | (col == GRID_COLS - 1)

    @pl.when(edge)
    def _():
        for ref in (stage_near, stage_far, sides_in, corners_in, rest_in):
            ref[...] = jnp.zeros_like(ref)

    barrier = pltpu.get_barrier_semaphore()
    for dr, dc in sides:

        @pl.when(has[dr, dc])
        def _(dr=dr, dc=dc):
            pl.semaphore_signal(
                barrier, inc=1, device_id={"row": row + dr, "col": col + dc}, device_id_type=MESH
            )

    pl.semaphore_signal(barrier, inc=1, device_id={"cfg": 1 - cfg}, device_id_type=MESH)

    own = pltpu.make_async_copy(
        features.at[0], stage_own.at[:, pl.ds(LEFT, COLS)], load_sem
    )
    own.start()
    small = []
    for n, (source, dest) in enumerate(
        (
            (gain_in, gain),
            (shift_in, shift),
            (mean_in, mean),
            (var_in, var),
            (bias_in, bias),
            (emb_in, emb),
            (out_weight_in, out_weight),
            (latent_in, latent),
            (guidance_in, guidance),
            (timestep_in, timestep),
            (coeffs_in, coeffs),
            (out_bias_in, out_bias),
        )
    ):
        load = pltpu.make_async_copy(source, dest, small_sem.at[n])
        load.start()
        small.append(load)
    early, small = small[:7], small[7:]
    loads = []
    for n in range(4):
        load = pltpu.make_async_copy(weight.at[n // 2, n % 2], wraw.at[n], wsem.at[n])
        load.start()
        loads.append(load)

    own.wait()
    for n in range(ROWS):
        cells = slice(n * STRIP, (n + 1) * STRIP)
        strips[0, cells] = stage_own[n, LEFT : LEFT + STRIP]
        strips[1, cells] = stage_own[n, LEFT + COLS - STRIP : LEFT + COLS]
    for n in range(HALO):
        for side in range(2):
            r = n + side * (ROWS - HALO)
            for half in range(2):
                begin = LEFT + half * COLS // 2
                rest_out[side, n, :, half * REST : (half + 1) * REST] = stage_own[
                    r, begin : begin + COLS // 2, MAIN:C
                ]

    arrivals = sum(jnp.where(has[s], 1, 0) for s in sides) + 1
    pl.semaphore_wait(barrier, arrivals)

    copies = []

    def send(dr, dc, source, dest):
        n = len(copies)
        copy = pltpu.make_async_remote_copy(
            src_ref=source,
            dst_ref=dest,
            send_sem=send_sem.at[n],
            recv_sem=recv_sem.at[n],
            device_id={"row": row + dr, "col": col + dc},
            device_id_type=MESH,
        )
        copies.append((copy, has[dr, dc], has[-dr, -dc]))

        @pl.when(has[dr, dc])
        def _():
            copy.start()

        return n

    def arrived(n):
        copy, _, comes = copies[n]

        @pl.when(comes)
        def _():
            copy.wait_recv()

    waits = ([], [], [])
    for dc in (-1, 1):
        waits[0].append(send(0, dc, strips.at[(1 + dc) // 2], sides_in.at[(1 - dc) // 2]))

    def send_rows(part):
        place = 0
        for first, count, side in PARTS[part]:
            row_out = first + ROWS - HALO if side < 0 else first - ROWS - HALO
            line = pl.ds(first if side < 0 else first - ROWS - HALO, count)
            stage = (stage_own, stage_near, stage_far)[part]
            source = features.at[0, pl.ds(row_out, count), :, pl.ds(0, MAIN)]
            dest = stage.at[pl.ds(place, count), pl.ds(LEFT, COLS), pl.ds(0, MAIN)]
            waits[part].append(send(-side, 0, source, dest))
            place += count
            source = rest_out.at[(1 - side) // 2, line]
            dest = rest_in.at[(1 + side) // 2, line]
            waits[part].append(send(-side, 0, source, dest))

    send_rows(1)
    for dr in (-1, 1):
        for dc in (-1, 1):
            cells = pl.ds(0, CORNER) if dr < 0 else pl.ds(ROWS * STRIP - CORNER, CORNER)
            n = send(
                dr,
                dc,
                strips.at[(1 + dc) // 2, cells],
                corners_in.at[(1 - dr) // 2, (1 - dc) // 2],
            )
            waits[1].append(n)
    send_rows(2)

    for load in early:
        load.wait()
    groups = lax.broadcasted_iota(jnp.int32, (GROUPS, C), 0)
    channels = lax.broadcasted_iota(jnp.int32, (GROUPS, C), 1)
    lowest = groups * (C // GROUPS)
    spread = jnp.where((channels >= lowest) & (channels < lowest + C // GROUPS), 1.0, 0.0).astype(F32)

    def to_channels(value):
        total = None
        for part in exact_parts(value):
            term = jnp.dot(part, spread, preferred_element_type=F32)
            total = term if total is None else total + term
        return total

    scale = to_channels(lax.rsqrt(var[:, 0, :] + NORM_EPS)) * gain[...]
    offset = shift[...] - to_channels(mean[:, 0, :]) * scale
    params[...] = jnp.zeros_like(params)
    for n in range(5):
        add = offset[n : n + 1]
        if n in (1, 3):
            k = n // 2
            add = add + scale[n : n + 1] * (bias[k, 0:1] + emb[0, k : k + 1])
        params[A_COL + n : A_COL + n + 1, 0:C] = 0.5 * scale[n : n + 1]
        params[B_COL + n : B_COL + n + 1, 0:C] = 0.5 * add
    for k in range(2):
        params[BIAS_COL + k : BIAS_COL + k + 1, 0:C] = bias[k, 1:2]
    turned_params = jnp.transpose(params[...])
    for n in range(12):
        pcols[n] = jnp.broadcast_to(turned_params[0:C, n : n + 1], (C, LANES))

    wout[...] = jnp.zeros_like(wout)
    for t in range(9):
        wout[8 * t : 8 * t + 4, :] = out_weight[t].astype(F32)

    for n in range(5):
        cell = lax.broadcasted_iota(jnp.int32, (8, masks.shape[2]), 1) + n * STEP
        cell_row = lax.shift_right_logical(cell * 28340, 21)
        cell_col = cell - cell_row * WIDE
        grid_row = cell_row + (row * ROWS - HALO)
        grid_col = cell_col + (col * COLS - HALO)
        inside = (
            (grid_row >= 0)
            & (grid_row < GRID_ROWS * ROWS)
            & (grid_col >= 0)
            & (grid_col < GRID_COLS * COLS)
        )
        masks[n] = jnp.where(inside, 1.0, 0.0).astype(F32)

    eye_row = lax.broadcasted_iota(jnp.int32, (C, C), 0)
    eye_col = lax.broadcasted_iota(jnp.int32, (C, C), 1)
    eye = jnp.where(eye_row == eye_col, 1.0, 0.0).astype(BF)

    def flipped(value):
        return lax.dot_general(
            eye, value, (((1,), (1,)), ((), ())), preferred_element_type=F32
        ).astype(BF)

    for n in range(4):
        loads[n].wait()

        @pl.loop(0, 1)
        def _(_, n=n):
            wflat[n] = flipped(wraw[n].reshape(9 * C, C))

    def silu(dest, values, norm, frame, first):
        for n in range(values.shape[1] // LANES):
            part = slice(n * LANES, (n + 1) * LANES)
            place = slice(first + n * LANES, first + (n + 1) * LANES)
            half = values[:, part] * pcols[A_COL + norm] + pcols[B_COL + norm]
            masked = half * masks[frame, 0:1, place]
            dest[:, place] = (masked * (1.0 + jnp.tanh(half))).astype(BF)

    def take(part):
        for n in waits[part]:
            arrived(n)
        ref = (stage_own, stage_near, stage_far)[part]
        places = []
        for first, count, side in PARTS[part]:
            for n in range(count):
                at = len(places)
                for half, place in ((0, LEFT - STRIP), (1, LEFT + COLS)):
                    if side == 0:
                        cells = sides_in[half, n * STRIP : (n + 1) * STRIP]
                    else:
                        line = first + n if side < 0 else first + n - HALO - ROWS
                        r = line + 1 if side < 0 else line
                        cells = corners_in[(1 + side) // 2, half, r * STRIP : (r + 1) * STRIP]
                    ref[at, place : place + STRIP] = cells
                for half in range(2 if side else 0):
                    begin = LEFT + half * COLS // 2
                    ref[at, begin : begin + COLS // 2, MAIN:C] = rest_in[
                        (1 + side) // 2, line, :, half * REST : (half + 1) * REST
                    ]
                places.append(first + n)
        turned = flipped(ref[...].reshape(len(places) * STAGE, C))
        for at, n in enumerate(places):
            begin = at * STAGE + LEFT - HALO
            hid_a[:, n * WIDE : (n + 1) * WIDE] = turned[:, begin : begin + WIDE]

    def first_act(begin, end):
        silu(act_a, hid_a[:, begin:end].astype(F32), 0, 0, begin)

    def gather(source, begin, end):
        for p in range(3):
            for q in range(3):
                tap = 3 * p + q
                shift_by = p * WIDE + q
                wide = end - begin + -(-shift_by // LANES) * LANES
                cells = source[:, begin : begin + wide]
                if shift_by:
                    cells = pltpu.roll(cells, wide - shift_by, 1)
                patches[tap * C : (tap + 1) * C, begin:end] = cells[:, 0 : end - begin]

    def product(layer, n, finish):
        part = slice(n * TILE, min((n + 1) * TILE, SIZES[layer]))
        finish(part, jnp.dot(wflat[layer], patches[:, part], preferred_element_type=F32))

    def conv(layer, source, finish):
        gather(source, 0, SIZES[layer])
        for n in range(-(-SIZES[layer] // TILE)):
            product(layer, n, finish)

    def inner(layer, dest):
        def finish(part, total):
            silu(dest, total, layer + 1, layer + 1, part.start)

        return finish

    def outer(layer, before, after, dest):
        k = layer // 2

        def finish(part, total):
            for n in range(total.shape[1] // LANES):
                place = slice(part.start + n * LANES, part.start + (n + 1) * LANES)
                skip = before[:, place].astype(F32)
                inc = total[:, n * LANES : (n + 1) * LANES] + pcols[BIAS_COL + k]
                hidden = (skip + inc).astype(BF)
                if after is not None:
                    after[:, place] = hidden
                silu(dest, hidden.astype(F32), layer + 1, layer + 1, place.start)

        return finish

    def shifted(dest, source, layer):
        size = SIZES[layer]
        dest[:, 0:size] = source[:, 2 * STEP : 2 * STEP + size]

    hid_a[:, TALL * WIDE :] = jnp.zeros((C, hid_a.shape[1] - TALL * WIDE), BF)
    finish = inner(0, act_b)
    take(0)
    first_act(384, 1280)
    gather(act_a, 512, 1024)
    product(0, 2, finish)
    product(0, 3, finish)
    take(1)
    first_act(256, 384)
    first_act(1152, 1536)
    gather(act_a, 256, 512)
    gather(act_a, 1024, 1280)
    product(0, 1, finish)
    product(0, 4, finish)
    take(2)
    first_act(0, 256)
    first_act(1408, 1792)
    gather(act_a, 0, 256)
    gather(act_a, 1280, 1536)
    product(0, 0, finish)
    product(0, 5, finish)
    shifted(hid_s, hid_a, 1)
    conv(1, act_b, outer(1, hid_s, hid_b, act_a))
    conv(2, act_a, inner(2, act_b))
    shifted(hid_s, hid_b, 3)
    conv(3, act_b, outer(3, hid_s, None, act_a))

    for load in small:
        load.wait()
    size = eps.shape[2]
    taps[...] = jnp.dot(wout[...].astype(BF), act_a[:, 0 : taps.shape[1]], preferred_element_type=F32)
    total = None
    for p in range(3):
        for q in range(3):
            t = 3 * p + q
            begin = p * WIDE + q
            term = taps[8 * t : 8 * t + 8, begin : begin + size]
            total = term if total is None else total + term
    for o in range(4):
        eps[o // 2, o % 2 : o % 2 + 1, :] = total[o : o + 1] + out_bias[o]

    swap = pltpu.make_async_remote_copy(
        src_ref=eps.at[1 - cfg],
        dst_ref=partner,
        send_sem=cfg_send,
        recv_sem=cfg_recv,
        device_id={"cfg": 1 - cfg},
        device_id_type=MESH,
    )
    swap.start()
    for copy, goes, _ in copies:

        @pl.when(goes)
        def _(copy=copy):
            copy.wait_send()

    swap.wait()
    mine, other = eps[cfg], partner[...]
    uncond = jnp.where(cfg == 1, other, mine)
    cond = jnp.where(cfg == 1, mine, other)
    guided = uncond + guidance[0] * (cond - uncond)
    step = timestep[0]
    c_latent, c_guided = coeffs[0, step], coeffs[1, step]
    for n in range(ROWS):
        out[n] = c_latent * latent[n] + c_guided * guided[:, n * WIDE : n * WIDE + COLS]


def per_device(
    features,
    latent,
    conv_weight,
    conv_bias,
    norm_gain,
    norm_shift,
    emb_shift,
    stale_mean,
    stale_var,
    out_weight,
    out_bias,
    guidance,
    timestep,
    coeffs,
):
    hbm = pl.BlockSpec(memory_space=pl.ANY)
    vmem = pl.BlockSpec(memory_space=pltpu.VMEM)
    dma = pltpu.SemaphoreType.DMA
    lanes = 1792
    def swapped(value):
        return jnp.transpose(value, (1, 0, 2))

    result = pl.pallas_call(
        kernel,
        out_shape=pltpu.VMEM((ROWS, 2, COLS), F32),
        in_specs=[hbm] * 14,
        out_specs=vmem,
        scratch_shapes=[
            pltpu.VMEM((ROWS, STAGE, C), BF),
            pltpu.VMEM((HALO, STAGE, C), BF),
            pltpu.VMEM((HALO, STAGE, C), BF),
            pltpu.VMEM((2, ROWS * STRIP, C), BF),
            pltpu.VMEM((2, ROWS * STRIP, C), BF),
            pltpu.VMEM((2, 2, CORNER, C), BF),
            pltpu.VMEM((2, HALO, COLS // 2, 2 * REST), BF),
            pltpu.VMEM((2, HALO, COLS // 2, 2 * REST), BF),
            pltpu.SMEM((1,), F32),
            pltpu.SMEM((1,), jnp.int32),
            pltpu.SMEM((2, 50), F32),
            pltpu.SMEM((4,), F32),
            pltpu.VMEM((ROWS, 2, COLS), F32),
            pltpu.VMEM((2, 2, C), F32),
            pltpu.VMEM((5, C), F32),
            pltpu.VMEM((5, C), F32),
            pltpu.VMEM((1, 2, C), F32),
            pltpu.VMEM((5, 1, GROUPS), F32),
            pltpu.VMEM((5, 1, GROUPS), F32),
            pltpu.VMEM((9, 4, C), BF),
            dma((12,)),
            pltpu.VMEM((4, 9, C, C), BF),
            pltpu.VMEM((4, C, 9 * C), BF),
            pltpu.VMEM((9 * C, SIZES[0]), BF),
            pltpu.VMEM((C, lanes), BF),
            pltpu.VMEM((C, lanes), BF),
            pltpu.VMEM((C, lanes), BF),
            pltpu.VMEM((C, lanes), BF),
            pltpu.VMEM((C, lanes), BF),
            pltpu.VMEM((128, 384), F32),
            pltpu.VMEM((12, C, LANES), F32),
            pltpu.VMEM((5, 8, lanes), F32),
            pltpu.VMEM((72, C), F32),
            pltpu.VMEM((72, 1152), F32),
            pltpu.VMEM((2, 2, 896), F32),
            pltpu.VMEM((2, 896), F32),
            dma,
            dma((4,)),
            dma((14,)),
            dma((14,)),
            dma,
            dma,
        ],
        compiler_params=pltpu.CompilerParams(
            collective_id=0, has_side_effects=True, vmem_limit_bytes=58 * 2**20
        ),
        cost_estimate=pl.CostEstimate(
            flops=12 * 10**9, bytes_accessed=10 * 2**20, transcendentals=2 * 10**6
        ),
    )(
        features,
        conv_weight,
        guidance,
        timestep,
        jnp.transpose(coeffs),
        out_bias,
        swapped(latent),
        conv_bias,
        norm_gain,
        norm_shift,
        emb_shift,
        swapped(stale_mean),
        swapped(stale_var),
        jnp.transpose(out_weight, (0, 2, 1)),
    )
    return swapped(result)


def solution(mesh):
    return jax.shard_map(
        per_device,
        mesh=mesh,
        in_specs=(
            P("cfg", "row", "col", None),
            P("cfg", "row", "col"),
            P(),
            P(),
            P(),
            P(),
            P("cfg", None, None),
            P("cfg", None, None),
            P("cfg", None, None),
            P(),
            P(),
            P(),
            P(),
            P(),
        ),
        out_specs=P("cfg", "row", "col"),
        check_vma=False,
    )
```

```python
import jax
import jax.numpy as jnp
from jax import lax
from jax.experimental import pallas as pl
from jax.experimental.pallas import tpu as pltpu
from jax.sharding import PartitionSpec as P

MESH = pl.DeviceIdType.MESH
BF, F32 = jnp.bfloat16, jnp.float32

C = 320
GROUPS = 32
ROWS, COLS = 12, 64
HALO = 5
WIDE = COLS + 2 * HALO
TALL = ROWS + 2 * HALO
STRIP = 8
LEFT = 16
STAGE = COLS + 2 * LEFT
CORNER = 6 * STRIP
PARTS = (((HALO, ROWS, 0),), ((0, HALO, -1), (HALO + ROWS, HALO, 1)))
STEP = WIDE + 1
TILE = 256
LANES = 128
SIZES = (1536, 1408, 1280, 1152)
GRID_ROWS, GRID_COLS = 16, 16
NORM_EPS = 1e-05
MAIN, REST = 256, 64

A_COL, B_COL, BIAS_COL = 0, 5, 10


def exact_parts(value):
    high = value.astype(BF).astype(F32)
    mid = (value - high).astype(BF).astype(F32)
    return high, mid, value - high - mid


def kernel(
    features,
    weight,
    guidance_in,
    timestep_in,
    coeffs_in,
    out_bias_in,
    latent_in,
    bias_in,
    gain_in,
    shift_in,
    emb_in,
    mean_in,
    var_in,
    out_weight_in,
    out,
    stage_own,
    stage_halo,
    strips,
    sides_in,
    corners_in,
    rest_out,
    rest_in,
    guidance,
    timestep,
    coeffs,
    out_bias,
    latent,
    bias,
    gain,
    shift,
    emb,
    mean,
    var,
    out_weight,
    small_sem,
    wraw,
    wflat,
    patches,
    act_a,
    act_b,
    hid_a,
    hid_b,
    hid_s,
    params,
    pcols,
    masks,
    wout,
    taps,
    eps,
    partner,
    load_sem,
    wsem,
    send_sem,
    recv_sem,
    cfg_send,
    cfg_recv,
):
    row, col, cfg = lax.axis_index("row"), lax.axis_index("col"), lax.axis_index("cfg")
    has = {
        (-1, 0): row > 0,
        (1, 0): row < GRID_ROWS - 1,
        (0, -1): col > 0,
        (0, 1): col < GRID_COLS - 1,
    }
    for dr in (-1, 1):
        for dc in (-1, 1):
            has[dr, dc] = has[dr, 0] & has[0, dc]
    sides = list(has)

    edge = (row == 0) | (row == GRID_ROWS - 1) | (col == 0) | (col == GRID_COLS - 1)

    @pl.when(edge)
    def _():
        for ref in (stage_halo, sides_in, corners_in, rest_in):
            ref[...] = jnp.zeros_like(ref)

    barrier = pltpu.get_barrier_semaphore()
    for dr, dc in sides:

        @pl.when(has[dr, dc])
        def _(dr=dr, dc=dc):
            pl.semaphore_signal(
                barrier, inc=1, device_id={"row": row + dr, "col": col + dc}, device_id_type=MESH
            )

    pl.semaphore_signal(barrier, inc=1, device_id={"cfg": 1 - cfg}, device_id_type=MESH)

    own = pltpu.make_async_copy(
        features.at[0], stage_own.at[:, pl.ds(LEFT, COLS)], load_sem
    )
    own.start()
    small = []
    for n, (source, dest) in enumerate(
        (
            (gain_in, gain),
            (shift_in, shift),
            (mean_in, mean),
            (var_in, var),
            (bias_in, bias),
            (emb_in, emb),
            (out_weight_in, out_weight),
            (latent_in, latent),
            (guidance_in, guidance),
            (timestep_in, timestep),
            (coeffs_in, coeffs),
            (out_bias_in, out_bias),
        )
    ):
        load = pltpu.make_async_copy(source, dest, small_sem.at[n])
        load.start()
        small.append(load)
    early, small = small[:7], small[7:]
    loads = []
    for n in range(4):
        load = pltpu.make_async_copy(weight.at[n // 2, n % 2], wraw.at[n], wsem.at[n])
        load.start()
        loads.append(load)

    for n in range(5):
        cell = lax.broadcasted_iota(jnp.int32, (8, masks.shape[2]), 1) + n * STEP
        cell_row = lax.shift_right_logical(cell * 28340, 21)
        cell_col = cell - cell_row * WIDE
        grid_row = cell_row + (row * ROWS - HALO)
        grid_col = cell_col + (col * COLS - HALO)
        inside = (
            (grid_row >= 0)
            & (grid_row < GRID_ROWS * ROWS)
            & (grid_col >= 0)
            & (grid_col < GRID_COLS * COLS)
        )
        masks[n] = jnp.where(inside, 1.0, 0.0).astype(F32)

    own.wait()
    for n in range(ROWS):
        cells = slice(n * STRIP, (n + 1) * STRIP)
        strips[0, cells] = stage_own[n, LEFT : LEFT + STRIP]
        strips[1, cells] = stage_own[n, LEFT + COLS - STRIP : LEFT + COLS]
    for n in range(HALO):
        for side in range(2):
            r = n + side * (ROWS - HALO)
            for half in range(2):
                begin = LEFT + half * COLS // 2
                rest_out[side, n, :, half * REST : (half + 1) * REST] = stage_own[
                    r, begin : begin + COLS // 2, MAIN:C
                ]

    for load in early:
        load.wait()
    groups = lax.broadcasted_iota(jnp.int32, (GROUPS, C), 0)
    channels = lax.broadcasted_iota(jnp.int32, (GROUPS, C), 1)
    lowest = groups * (C // GROUPS)
    spread = jnp.where((channels >= lowest) & (channels < lowest + C // GROUPS), 1.0, 0.0).astype(F32)

    def to_channels(value):
        total = None
        for part in exact_parts(value):
            term = jnp.dot(part, spread, preferred_element_type=F32)
            total = term if total is None else total + term
        return total

    scale = to_channels(lax.rsqrt(var[:, 0, :] + NORM_EPS)) * gain[...]
    offset = shift[...] - to_channels(mean[:, 0, :]) * scale
    params[...] = jnp.zeros_like(params)
    for n in range(5):
        add = offset[n : n + 1]
        if n in (1, 3):
            k = n // 2
            add = add + scale[n : n + 1] * (bias[k, 0:1] + emb[0, k : k + 1])
        params[A_COL + n : A_COL + n + 1, 0:C] = 0.5 * scale[n : n + 1]
        params[B_COL + n : B_COL + n + 1, 0:C] = 0.5 * add
    for k in range(2):
        params[BIAS_COL + k : BIAS_COL + k + 1, 0:C] = bias[k, 1:2]
    turned_params = jnp.transpose(params[...])
    for n in range(12):
        pcols[n] = jnp.broadcast_to(turned_params[0:C, n : n + 1], (C, LANES))

    wout[...] = jnp.zeros_like(wout)
    for t in range(9):
        wout[8 * t : 8 * t + 4, :] = out_weight[t].astype(F32)

    arrivals = sum(jnp.where(has[s], 1, 0) for s in sides) + 1
    pl.semaphore_wait(barrier, arrivals)

    copies = []

    def send(dr, dc, source, dest):
        n = len(copies)
        copy = pltpu.make_async_remote_copy(
            src_ref=source,
            dst_ref=dest,
            send_sem=send_sem.at[n],
            recv_sem=recv_sem.at[n],
            device_id={"row": row + dr, "col": col + dc},
            device_id_type=MESH,
        )
        copies.append((copy, has[dr, dc], has[-dr, -dc]))

        @pl.when(has[dr, dc])
        def _():
            copy.start()

        return n

    def arrived(n):
        copy, _, comes = copies[n]

        @pl.when(comes)
        def _():
            copy.wait_recv()

    waits = ([], [])
    for dc in (-1, 1):
        waits[0].append(send(0, dc, strips.at[(1 + dc) // 2], sides_in.at[(1 - dc) // 2]))
    for dr in (-1, 1):
        for dc in (-1, 1):
            cells = pl.ds(0, CORNER) if dr < 0 else pl.ds(ROWS * STRIP - CORNER, CORNER)
            n = send(
                dr,
                dc,
                strips.at[(1 + dc) // 2, cells],
                corners_in.at[(1 - dr) // 2, (1 - dc) // 2],
            )
            waits[1].append(n)
    for dr in (-1, 1):
        n = send(dr, 0, rest_out.at[(1 + dr) // 2], rest_in.at[(1 - dr) // 2])
        waits[1].append(n)
    for dr in (-1, 1):
        begin = 0 if dr < 0 else ROWS - HALO
        n = send(
            dr,
            0,
            features.at[0, pl.ds(begin, HALO), :, pl.ds(0, MAIN)],
            stage_halo.at[pl.ds(HALO if dr < 0 else 0, HALO), pl.ds(LEFT, COLS), pl.ds(0, MAIN)],
        )
        waits[1].append(n)

    eye_row = lax.broadcasted_iota(jnp.int32, (C, C), 0)
    eye_col = lax.broadcasted_iota(jnp.int32, (C, C), 1)
    eye = jnp.where(eye_row == eye_col, 1.0, 0.0).astype(BF)

    def flipped(value):
        return lax.dot_general(
            eye, value, (((1,), (1,)), ((), ())), preferred_element_type=F32
        ).astype(BF)

    for n in range(4):
        loads[n].wait()

        @pl.loop(0, 1)
        def _(_, n=n):
            wflat[n] = flipped(wraw[n].reshape(9 * C, C))

    def silu(dest, values, norm, frame, first):
        for n in range(values.shape[1] // LANES):
            part = slice(n * LANES, (n + 1) * LANES)
            place = slice(first + n * LANES, first + (n + 1) * LANES)
            half = values[:, part] * pcols[A_COL + norm] + pcols[B_COL + norm]
            masked = half * masks[frame, 0:1, place]
            dest[:, place] = (masked * (1.0 + jnp.tanh(half))).astype(BF)

    def take(part):
        for n in waits[part]:
            arrived(n)
        ref = (stage_own, stage_halo)[part]
        places = []
        for first, count, side in PARTS[part]:
            for n in range(count):
                at = len(places)
                for half, place in ((0, LEFT - STRIP), (1, LEFT + COLS)):
                    if side == 0:
                        cells = sides_in[half, n * STRIP : (n + 1) * STRIP]
                    else:
                        r = n + 1 if side < 0 else n
                        cells = corners_in[(1 + side) // 2, half, r * STRIP : (r + 1) * STRIP]
                    ref[at, place : place + STRIP] = cells
                for half in range(2 if side else 0):
                    begin = LEFT + half * COLS // 2
                    ref[at, begin : begin + COLS // 2, MAIN:C] = rest_in[
                        (1 + side) // 2, n, :, half * REST : (half + 1) * REST
                    ]
                places.append(first + n)
        turned = flipped(ref[...].reshape(len(places) * STAGE, C))
        for at, n in enumerate(places):
            begin = at * STAGE + LEFT - HALO
            hid_a[:, n * WIDE : (n + 1) * WIDE] = turned[:, begin : begin + WIDE]

    def first_act(begin, end):
        silu(act_a, hid_a[:, begin:end].astype(F32), 0, 0, begin)

    def gather(source, begin, end):
        for p in range(3):
            for q in range(3):
                tap = 3 * p + q
                shift_by = p * WIDE + q
                wide = end - begin + -(-shift_by // LANES) * LANES
                cells = source[:, begin : begin + wide]
                if shift_by:
                    cells = pltpu.roll(cells, wide - shift_by, 1)
                patches[tap * C : (tap + 1) * C, begin:end] = cells[:, 0 : end - begin]

    def product(layer, n, finish):
        part = slice(n * TILE, min((n + 1) * TILE, SIZES[layer]))
        finish(part, jnp.dot(wflat[layer], patches[:, part], preferred_element_type=F32))

    def conv(layer, source, finish):
        gather(source, 0, SIZES[layer])
        for n in range(-(-SIZES[layer] // TILE)):
            product(layer, n, finish)

    def inner(layer, dest):
        def finish(part, total):
            silu(dest, total, layer + 1, layer + 1, part.start)

        return finish

    def outer(layer, before, after, dest):
        k = layer // 2

        def finish(part, total):
            for n in range(total.shape[1] // LANES):
                place = slice(part.start + n * LANES, part.start + (n + 1) * LANES)
                skip = before[:, place].astype(F32)
                inc = total[:, n * LANES : (n + 1) * LANES] + pcols[BIAS_COL + k]
                hidden = (skip + inc).astype(BF)
                if after is not None:
                    after[:, place] = hidden
                silu(dest, hidden.astype(F32), layer + 1, layer + 1, place.start)

        return finish

    def shifted(dest, source, layer):
        size = SIZES[layer]
        wide = size + 2 * LANES
        cells = pltpu.roll(source[:, 0:wide], wide - 2 * STEP, 1)
        dest[:, 0:size] = cells[:, 0:size]

    hid_a[:, TALL * WIDE :] = jnp.zeros((C, hid_a.shape[1] - TALL * WIDE), BF)
    finish = inner(0, act_b)
    take(0)
    first_act(384, 1280)
    gather(act_a, 512, 1024)
    product(0, 2, finish)
    product(0, 3, finish)
    take(1)
    first_act(0, 384)
    first_act(1152, 1792)
    gather(act_a, 0, 512)
    gather(act_a, 1024, 1536)
    for n in (0, 1, 4, 5):
        product(0, n, finish)
    shifted(hid_s, hid_a, 1)
    conv(1, act_b, outer(1, hid_s, hid_b, act_a))
    conv(2, act_a, inner(2, act_b))
    shifted(hid_s, hid_b, 3)
    conv(3, act_b, outer(3, hid_s, None, act_a))

    for load in small:
        load.wait()
    size = eps.shape[2]
    taps[...] = jnp.dot(wout[...].astype(BF), act_a[:, 0 : taps.shape[1]], preferred_element_type=F32)
    total = None
    for p in range(3):
        for q in range(3):
            t = 3 * p + q
            begin = p * WIDE + q
            term = taps[8 * t : 8 * t + 8, begin : begin + size]
            total = term if total is None else total + term
    for o in range(4):
        eps[o // 2, o % 2 : o % 2 + 1, :] = total[o : o + 1] + out_bias[o]

    swap = pltpu.make_async_remote_copy(
        src_ref=eps.at[1 - cfg],
        dst_ref=partner,
        send_sem=cfg_send,
        recv_sem=cfg_recv,
        device_id={"cfg": 1 - cfg},
        device_id_type=MESH,
    )
    swap.start()
    for copy, goes, _ in copies:

        @pl.when(goes)
        def _(copy=copy):
            copy.wait_send()

    swap.wait()
    mine, other = eps[cfg], partner[...]
    uncond = jnp.where(cfg == 1, other, mine)
    cond = jnp.where(cfg == 1, mine, other)
    guided = uncond + guidance[0] * (cond - uncond)
    step = timestep[0]
    c_latent, c_guided = coeffs[0, step], coeffs[1, step]
    for n in range(ROWS):
        out[n] = c_latent * latent[n] + c_guided * guided[:, n * WIDE : n * WIDE + COLS]


def per_device(
    features,
    latent,
    conv_weight,
    conv_bias,
    norm_gain,
    norm_shift,
    emb_shift,
    stale_mean,
    stale_var,
    out_weight,
    out_bias,
    guidance,
    timestep,
    coeffs,
):
    hbm = pl.BlockSpec(memory_space=pl.ANY)
    vmem = pl.BlockSpec(memory_space=pltpu.VMEM)
    dma = pltpu.SemaphoreType.DMA
    lanes = 1792
    def swapped(value):
        return jnp.transpose(value, (1, 0, 2))

    result = pl.pallas_call(
        kernel,
        out_shape=pltpu.VMEM((ROWS, 2, COLS), F32),
        in_specs=[hbm] * 14,
        out_specs=vmem,
        scratch_shapes=[
            pltpu.VMEM((ROWS, STAGE, C), BF),
            pltpu.VMEM((2 * HALO, STAGE, C), BF),
            pltpu.VMEM((2, ROWS * STRIP, C), BF),
            pltpu.VMEM((2, ROWS * STRIP, C), BF),
            pltpu.VMEM((2, 2, CORNER, C), BF),
            pltpu.VMEM((2, HALO, COLS // 2, 2 * REST), BF),
            pltpu.VMEM((2, HALO, COLS // 2, 2 * REST), BF),
            pltpu.SMEM((1,), F32),
            pltpu.SMEM((1,), jnp.int32),
            pltpu.SMEM((2, 50), F32),
            pltpu.SMEM((4,), F32),
            pltpu.VMEM((ROWS, 2, COLS), F32),
            pltpu.VMEM((2, 2, C), F32),
            pltpu.VMEM((5, C), F32),
            pltpu.VMEM((5, C), F32),
            pltpu.VMEM((1, 2, C), F32),
            pltpu.VMEM((5, 1, GROUPS), F32),
            pltpu.VMEM((5, 1, GROUPS), F32),
            pltpu.VMEM((9, 4, C), BF),
            dma((12,)),
            pltpu.VMEM((4, 9, C, C), BF),
            pltpu.VMEM((4, C, 9 * C), BF),
            pltpu.VMEM((9 * C, SIZES[0]), BF),
            pltpu.VMEM((C, lanes), BF),
            pltpu.VMEM((C, lanes), BF),
            pltpu.VMEM((C, lanes), BF),
            pltpu.VMEM((C, lanes), BF),
            pltpu.VMEM((C, lanes), BF),
            pltpu.VMEM((128, 384), F32),
            pltpu.VMEM((12, C, LANES), F32),
            pltpu.VMEM((5, 8, lanes), F32),
            pltpu.VMEM((72, C), F32),
            pltpu.VMEM((72, 1152), F32),
            pltpu.VMEM((2, 2, 896), F32),
            pltpu.VMEM((2, 896), F32),
            dma,
            dma((4,)),
            dma((10,)),
            dma((10,)),
            dma,
            dma,
        ],
        compiler_params=pltpu.CompilerParams(
            collective_id=0, has_side_effects=True, vmem_limit_bytes=58 * 2**20
        ),
        cost_estimate=pl.CostEstimate(
            flops=12 * 10**9, bytes_accessed=10 * 2**20, transcendentals=2 * 10**6
        ),
    )(
        features,
        conv_weight,
        guidance,
        timestep,
        jnp.transpose(coeffs),
        out_bias,
        swapped(latent),
        conv_bias,
        norm_gain,
        norm_shift,
        emb_shift,
        swapped(stale_mean),
        swapped(stale_var),
        jnp.transpose(out_weight, (0, 2, 1)),
    )
    return swapped(result)


def solution(mesh):
    return jax.shard_map(
        per_device,
        mesh=mesh,
        in_specs=(
            P("cfg", "row", "col", None),
            P("cfg", "row", "col"),
            P(),
            P(),
            P(),
            P(),
            P("cfg", None, None),
            P("cfg", None, None),
            P("cfg", None, None),
            P(),
            P(),
            P(),
            P(),
            P(),
        ),
        out_specs=P("cfg", "row", "col"),
        check_vma=False,
    )
```
